256 devices in a mesh: seq: 16 (over x_lo, y, core), dp: 16 (over x_hi, z).
Axes of the slice: x: 4 (x_hi: 2, x_lo: 2; x = x_hi * 2 + x_lo), y: 4, z: 8, core: 2. Of those that a mesh axis runs over, the one named last changes fastest.
Arguments:
- normed: bfloat16 [16, 4096, 8192], P('dp', 'seq'), may hold values from -6 to 6
- query_frozen: bfloat16 [16, 4096, 4096], P('dp', 'seq'), may hold values from -64 to 64
- key_projected: bfloat16 [16, 4096, 512], P('dp', 'seq'), may hold values from -4.5 to 4.5
- value_frozen: bfloat16 [16, 4096, 512], P('dp', 'seq'), may hold values from -6 to 6
- query_down_weight: bfloat16 [8192, 16], replicated, may hold values from -0.0625 to 0.0625
- query_up_weight: bfloat16 [16, 4096], replicated, may hold values from -1.5 to 1.5
- value_down_weight: bfloat16 [8192, 16], replicated, may hold values from -0.0625 to 0.0625
- value_up_weight: bfloat16 [16, 512], replicated, may hold values from -1.5 to 1.5
- output_cotangent: bfloat16 [16, 4096, 4096], P('dp', 'seq'), may hold values from -6 to 6
Outputs:
- attn_output: bfloat16 [16, 4096, 4096], P('dp', 'seq')
- grad_aq: float32 [8192, 16], replicated
- grad_bq: float32 [16, 4096], replicated
- grad_av: float32 [8192, 16], replicated
- grad_bv: float32 [16, 512], replicated
The draws below stay inside these ranges and needn't reach their ends.
All inputs are finite; a program needn't handle non-finite values.
Results may differ from the reference program's by a relative error of at most 0.012.
The reference program's roundings to bfloat16 on the way count: a program that leaves them out, or rounds other values in their place, can miss the bound.
Values may be sent and summed in bfloat16 or wider, within the bound.
No kernel may reach another device: no remote copies, remote signals or barrier semaphores. Data moves between devices by JAX's collectives and lax.ppermute only.
A program may use at most 64 MiB of HBM per device.

```python
import math
import jax
import jax.numpy as jnp
from jax import lax

MODEL_WIDTH = 8192
QUERY_HEADS = 32
KEY_VALUE_HEADS = 4
HEAD_FEATURES = 128
ADAPTER_RANK = 16
SEQUENCE_COUNT = 16
SEQUENCE_LENGTH = 4096
GROUP = 512
SHIFT = 256


def shared_keys(key):
    shape = (SEQUENCE_COUNT, SEQUENCE_LENGTH, KEY_VALUE_HEADS * HEAD_FEATURES)
    raw = jax.random.normal(jax.random.fold_in(key, 1), shape, jnp.float32)
    return raw


def draw_key_projected(key, part):
    raw = shared_keys(key)
    return jnp.clip(raw, -4.5, 4.5).astype(jnp.bfloat16)


def draw_query_frozen(key, part):
    shape = (SEQUENCE_COUNT, SEQUENCE_LENGTH, QUERY_HEADS * HEAD_FEATURES)
    key = jax.random.fold_in(key, 17)
    return jnp.clip(jax.random.normal(key, shape, jnp.float32), -4.5, 4.5).astype(jnp.bfloat16)


def level_of(own_key, shape, cuts, smallest, largest):
    factor_of, own = 1.0, jax.random.fold_in(own_key, 6)
    for dim, parts in cuts:
        draws = jnp.exp(jax.random.uniform(jax.random.fold_in(own, dim), (parts,), jnp.float32, smallest / len(cuts), largest / len(cuts)))
        factor_of = factor_of * jnp.repeat(draws, shape[dim] // parts).reshape([-1 if axis == dim else 1 for axis in range(len(shape))])
    return factor_of


def bell_draw(own_key, extent, deviation, limit, split=(), held_as=jnp.bfloat16):
    result = deviation * jax.random.normal(own_key, extent, jnp.float32)
    if split:
        result = result * level_of(own_key, extent, split, -0.22, 0.18)
    return jnp.clip(result, -limit, limit).astype(held_as)


def setup_inputs(seed: int = 0) -> dict:
    arg_keys = jax.random.split(jax.random.key(seed), 10)
    normed = bell_draw(arg_keys[0], (SEQUENCE_COUNT, SEQUENCE_LENGTH, MODEL_WIDTH), 1.0, 6.0, ((0, 16), (1, 16)))
    query_frozen = draw_query_frozen(jax.random.fold_in(arg_keys[9], 71), 0)
    key_projected = draw_key_projected(jax.random.fold_in(arg_keys[9], 71), 0)
    value_frozen = bell_draw(arg_keys[3], (SEQUENCE_COUNT, SEQUENCE_LENGTH, KEY_VALUE_HEADS * HEAD_FEATURES), 1.0, 6.0, ((0, 16), (1, 16)))
    query_down_weight = bell_draw(arg_keys[4], (MODEL_WIDTH, ADAPTER_RANK), MODEL_WIDTH ** -0.5, 0.0625)
    query_up_weight = bell_draw(arg_keys[5], (ADAPTER_RANK, QUERY_HEADS * HEAD_FEATURES), ADAPTER_RANK ** -0.5, 1.5)
    value_down_weight = bell_draw(arg_keys[6], (MODEL_WIDTH, ADAPTER_RANK), MODEL_WIDTH ** -0.5, 0.0625)
    value_up_weight = bell_draw(arg_keys[7], (ADAPTER_RANK, KEY_VALUE_HEADS * HEAD_FEATURES), ADAPTER_RANK ** -0.5, 1.5)
    output_cotangent = bell_draw(arg_keys[8], (SEQUENCE_COUNT, SEQUENCE_LENGTH, QUERY_HEADS * HEAD_FEATURES), 1.0, 6.0, ((0, 16), (1, 16)))
    return {"normed": normed, "query_frozen": query_frozen, "key_projected": key_projected, "value_frozen": value_frozen, "query_down_weight": query_down_weight, "query_up_weight": query_up_weight, "value_down_weight": value_down_weight, "value_up_weight": value_up_weight, "output_cotangent": output_cotangent}


adapter_scale = 2.0
masked_score = -1e+30

def group_attention(q_rows, keys, values, dout_rows, per_key):
    rows = q_rows.shape[1]
    width = keys.shape[1]
    query_place = lax.broadcasted_iota(jnp.int32, (rows, width), 0) // per_key
    key_place = lax.broadcasted_iota(jnp.int32, (rows, width), 1)
    visible = key_place <= query_place
    inv_root = 1.0 / math.sqrt(q_rows.shape[2])
    query_f = q_rows.astype(jnp.float32)
    keys_f = keys.astype(jnp.float32)
    values_f = values.astype(jnp.float32)
    dout_f = dout_rows.astype(jnp.float32)
    score = jnp.einsum('nre,nse->nrs', query_f, keys_f) * inv_root
    score = jnp.where(visible[None], score, masked_score)
    top = lax.optimization_barrier(jnp.max(score, axis=2, keepdims=True))
    expo = jnp.exp(score - top)
    prob = expo / lax.optimization_barrier(jnp.sum(expo, axis=2, keepdims=True))
    prob_b = lax.optimization_barrier(prob.astype(jnp.bfloat16)).astype(jnp.float32)
    attended = jnp.einsum('nrs,nse->nre', prob_b, values_f)
    delta = lax.optimization_barrier(jnp.sum(dout_f * attended, axis=2, keepdims=True))
    dprob = jnp.einsum('nre,nse->nrs', dout_f, values_f)
    dscore = lax.optimization_barrier((prob * (dprob - delta)).astype(jnp.bfloat16)).astype(jnp.float32)
    dquery = jnp.einsum('nrs,nse->nre', dscore, keys_f) * inv_root
    dvalue = jnp.einsum('nrs,nre->nse', prob_b, dout_f)
    return (attended.astype(jnp.bfloat16), dquery, dvalue)

def single_sequence(input_sequence, query_sequence, key_sequence, value_sequence, output_grad_sequence, query_down_weight, query_up_weight, value_down_weight, value_up_weight):
    per_key = QUERY_HEADS // KEY_VALUE_HEADS
    query_latent = jnp.dot(input_sequence, query_down_weight, preferred_element_type=jnp.float32).astype(jnp.bfloat16)
    query_tensor = (query_sequence.astype(jnp.float32) + adapter_scale * jnp.dot(query_latent, query_up_weight, preferred_element_type=jnp.float32)).astype(jnp.bfloat16)
    value_latent = jnp.dot(input_sequence, value_down_weight, preferred_element_type=jnp.float32).astype(jnp.bfloat16)
    value_tensor = (value_sequence.astype(jnp.float32) + adapter_scale * jnp.dot(value_latent, value_up_weight, preferred_element_type=jnp.float32)).astype(jnp.bfloat16)
    outs = []
    dqueries = []
    dvalues = []
    groups = SEQUENCE_LENGTH // GROUP
    for group in range(KEY_VALUE_HEADS):
        move = SHIFT if group >= KEY_VALUE_HEADS // 2 else 0
        qcols = slice(group * per_key * HEAD_FEATURES, (group + 1) * per_key * HEAD_FEATURES)
        kcols = slice(group * HEAD_FEATURES, (group + 1) * HEAD_FEATURES)
        q_rows = jnp.roll(query_tensor[:, qcols], -move, axis=0).reshape(groups, GROUP * per_key, HEAD_FEATURES)
        d_rows = jnp.roll(output_grad_sequence[:, qcols], -move, axis=0).reshape(groups, GROUP * per_key, HEAD_FEATURES)
        keys = jnp.roll(key_sequence[:, kcols], -move, axis=0).reshape(groups, GROUP, HEAD_FEATURES)
        values = jnp.roll(value_tensor[:, kcols], -move, axis=0).reshape(groups, GROUP, HEAD_FEATURES)
        attended, dquery, dvalue = group_attention(q_rows, keys, values, d_rows, per_key)
        outs.append(jnp.roll(attended.reshape(SEQUENCE_LENGTH, per_key * HEAD_FEATURES), move, axis=0))
        dqueries.append(jnp.roll(dquery.reshape(SEQUENCE_LENGTH, per_key * HEAD_FEATURES), move, axis=0))
        dvalues.append(jnp.roll(dvalue.reshape(SEQUENCE_LENGTH, HEAD_FEATURES), move, axis=0))
    attn_output = jnp.concatenate(outs, axis=1)
    query_up_gradient = jnp.concatenate(dqueries, axis=1).astype(jnp.bfloat16)
    value_up_gradient = jnp.concatenate(dvalues, axis=1).astype(jnp.bfloat16)
    query_up_term = jnp.dot(query_up_gradient, query_up_weight.T, preferred_element_type=jnp.float32).astype(jnp.bfloat16)
    value_up_term = jnp.dot(value_up_gradient, value_up_weight.T, preferred_element_type=jnp.float32).astype(jnp.bfloat16)
    term_aq = jnp.dot(input_sequence.T, query_up_term, preferred_element_type=jnp.float32)
    term_bq = jnp.dot(query_latent.T, query_up_gradient, preferred_element_type=jnp.float32)
    term_av = jnp.dot(input_sequence.T, value_up_term, preferred_element_type=jnp.float32)
    term_bv = jnp.dot(value_latent.T, value_up_gradient, preferred_element_type=jnp.float32)
    return (attn_output, term_aq, term_bq, term_av, term_bv)

def reference(normed, query_frozen, key_projected, value_frozen, query_down_weight, query_up_weight, value_down_weight, value_up_weight, output_cotangent):

    def per_seq(batch_items):
        return single_sequence(batch_items[0], batch_items[1], batch_items[2], batch_items[3], batch_items[4], query_down_weight, query_up_weight, value_down_weight, value_up_weight)
    attn_output, term_aq, term_bq, term_av, term_bv = lax.map(per_seq, (normed, query_frozen, key_projected, value_frozen, output_cotangent))
    scale_factor = adapter_scale / math.sqrt(SEQUENCE_COUNT * SEQUENCE_LENGTH)
    grad_aq = lax.optimization_barrier(jnp.sum(term_aq, axis=0)) * scale_factor
    grad_bq = lax.optimization_barrier(jnp.sum(term_bq, axis=0)) * scale_factor
    grad_av = lax.optimization_barrier(jnp.sum(term_av, axis=0)) * scale_factor
    grad_bv = lax.optimization_barrier(jnp.sum(term_bv, axis=0)) * scale_factor
    return (attn_output, grad_aq, grad_bq, grad_av, grad_bv)
```

```python
import math

import jax
import jax.numpy as jnp
from jax import lax
from jax.sharding import PartitionSpec as P

QUERY_HEADS = 32
KEY_VALUE_HEADS = 4
HEAD_FEATURES = 128


adapter_scale = 2.0
masked_score = -1e30


AXES = ("seq", "dp")
CORE_BIT = 16
PLANE_BITS = (32, 64, 128, 8)
DEPTH_BITS = (1, 2, 4)
CHUNKS = 32
CHUNK_ROWS = 96


def groups_of(bits, count):
    groups = []
    for base in range(count):
        if any(base & bit for bit in bits):
            continue
        members = []
        for code in range(1 << len(bits)):
            members.append(base + sum(bit for n, bit in enumerate(bits) if code >> n & 1))
        groups.append(members)
    return groups


def exchanged(value, bits):
    groups = groups_of(bits, lax.axis_size(AXES))
    return lax.all_to_all(value, AXES, 0, 0, axis_index_groups=groups)


def sum_over_first(value):
    return jnp.sum(value.astype(jnp.float32), axis=0)


def spread(value, bits):
    copies = jnp.broadcast_to(value[None], (1 << len(bits),) + value.shape)
    return exchanged(copies, bits)


def swapped(value, bit):
    count = lax.axis_size(AXES)
    return lax.ppermute(value, AXES, [(i, i ^ bit) for i in range(count)])


def packed(terms):
    flat = jnp.concatenate([term.reshape(-1) for term in terms])
    flat = jnp.pad(flat, (0, CHUNKS * CHUNK_ROWS * 128 - flat.shape[0]))
    return flat.reshape(CHUNKS, CHUNK_ROWS, 128)


def unpacked(chunks, shapes):
    flat = chunks.reshape(-1)
    parts, start = ([], 0)
    for rows, cols in shapes:
        parts.append(flat[start : start + rows * cols].reshape(rows, cols).astype(jnp.float32))
        start += rows * cols
    return parts


def summed(chunks):
    half = CHUNKS // 2
    core = lax.axis_index("seq") % 2
    kept = lax.dynamic_slice_in_dim(chunks, core * half, half, 0)
    given = lax.dynamic_slice_in_dim(chunks, (1 - core) * half, half, 0)
    halves = kept + swapped(given.astype(jnp.bfloat16), CORE_BIT).astype(jnp.float32)
    piece = sum_over_first(exchanged(halves.astype(jnp.bfloat16), PLANE_BITS))
    piece = sum_over_first(spread(piece.astype(jnp.bfloat16), DEPTH_BITS))
    whole_half = spread(piece.astype(jnp.bfloat16), PLANE_BITS)
    other_half = swapped(whole_half, CORE_BIT)
    first = jnp.where(core == 0, whole_half, other_half)
    second = jnp.where(core == 0, other_half, whole_half)
    return jnp.concatenate([first, second], axis=0)


def shifted(value, axis, by):
    devices = lax.axis_size(axis)
    return lax.ppermute(value, axis, [(i, (i + by) % devices) for i in range(devices)])


def attend_rows(q_rows, keys, values, dout_rows, per_key, prev_seen):
    rows = q_rows.shape[0]
    width = keys.shape[0]
    token_count = rows // per_key
    query_place = lax.broadcasted_iota(jnp.int32, (rows, width), 0) // per_key
    key_place = lax.broadcasted_iota(jnp.int32, (rows, width), 1) - (width - token_count)
    visible = key_place <= query_place
    visible = visible & ((key_place >= 0) | prev_seen)
    inv_root = 1.0 / math.sqrt(q_rows.shape[1])
    score = jnp.dot(q_rows, keys.T, preferred_element_type=jnp.float32) * inv_root
    score = jnp.where(visible, score, masked_score)
    top = jnp.max(score, axis=1, keepdims=True)
    expo = jnp.exp(score - top)
    prob = expo / jnp.sum(expo, axis=1, keepdims=True)
    prob_b = prob.astype(jnp.bfloat16)
    attended = jnp.dot(prob_b, values, preferred_element_type=jnp.float32)
    delta = jnp.sum(dout_rows.astype(jnp.float32) * attended, axis=1, keepdims=True)
    dprob = jnp.dot(dout_rows, values.T, preferred_element_type=jnp.float32)
    dscore = (prob * (dprob - delta)).astype(jnp.bfloat16)
    dquery = jnp.dot(dscore, keys, preferred_element_type=jnp.float32) * inv_root
    dvalue = jnp.einsum("rs,re->se", prob_b, dout_rows, preferred_element_type=jnp.float32)
    return (attended.astype(jnp.bfloat16), dquery, dvalue)


def head_rows(array, index, per_key):
    cols = per_key * HEAD_FEATURES
    return array[:, index * cols : (index + 1) * cols].reshape(-1, HEAD_FEATURES)


def on_device(
    normed,
    query_frozen,
    key_projected,
    value_frozen,
    query_down_weight,
    query_up_weight,
    value_down_weight,
    value_up_weight,
    output_cotangent,
):
    input_arrays = normed[0]
    token_count = input_arrays.shape[0]
    per_key = QUERY_HEADS // KEY_VALUE_HEADS
    half_kv = KEY_VALUE_HEADS // 2
    query_latent = jnp.dot(
        input_arrays, query_down_weight, preferred_element_type=jnp.float32
    ).astype(jnp.bfloat16)
    query_tensor = (
        query_frozen[0].astype(jnp.float32)
        + adapter_scale * jnp.dot(query_latent, query_up_weight, preferred_element_type=jnp.float32)
    ).astype(jnp.bfloat16)
    value_latent = jnp.dot(
        input_arrays, value_down_weight, preferred_element_type=jnp.float32
    ).astype(jnp.bfloat16)
    value_tensor = (
        value_frozen[0].astype(jnp.float32)
        + adapter_scale * jnp.dot(value_latent, value_up_weight, preferred_element_type=jnp.float32)
    ).astype(jnp.bfloat16)
    keys = key_projected[0]
    dout = output_cotangent[0]
    place = lax.axis_index("seq")
    second_place = place % 2 == 1
    send_k, send_v = (keys, value_tensor)
    prev_k, prev_v = shifted((send_k, send_v), "seq", 1)
    outs, dqueries, back_parts, own_parts = ([], [], [], [])
    for group in range(KEY_VALUE_HEADS):
        seen = second_place if group < half_kv else jnp.logical_not(second_place)
        cols = slice(group * HEAD_FEATURES, (group + 1) * HEAD_FEATURES)
        both_k = jnp.concatenate([prev_k[:, cols], keys[:, cols]], axis=0)
        both_v = jnp.concatenate([prev_v[:, cols], value_tensor[:, cols]], axis=0)
        attended, dquery, dvalue = attend_rows(
            head_rows(query_tensor, group, per_key),
            both_k,
            both_v,
            head_rows(dout, group, per_key),
            per_key,
            seen,
        )
        outs.append(attended.reshape(token_count, -1))
        dqueries.append(dquery.reshape(token_count, -1))
        back_parts.append(dvalue[:token_count])
        own_parts.append(dvalue[token_count:])
    out_rows = jnp.concatenate(outs, axis=1)
    dquery_all = jnp.concatenate(dqueries, axis=1)
    dv_back = jnp.concatenate(back_parts, axis=1)
    dvalue_own = jnp.concatenate(own_parts, axis=1)
    query_up_gradient = dquery_all.astype(jnp.bfloat16)
    query_up_term = jnp.einsum(
        "df,sf->ds", query_up_gradient, query_up_weight, preferred_element_type=jnp.float32
    ).astype(jnp.bfloat16)
    term_aq = jnp.einsum(
        "td,tr->dr", input_arrays, query_up_term, preferred_element_type=jnp.float32
    )
    term_bq = jnp.einsum(
        "tr,tc->rc", query_latent, query_up_gradient, preferred_element_type=jnp.float32
    )
    returned = shifted(dv_back, "seq", -1)
    dvalue_all = dvalue_own + returned
    value_up_gradient = dvalue_all.astype(jnp.bfloat16)
    value_up_term = jnp.einsum(
        "df,sf->ds", value_up_gradient, value_up_weight, preferred_element_type=jnp.float32
    ).astype(jnp.bfloat16)
    term_av = jnp.einsum(
        "td,tr->dr", input_arrays, value_up_term, preferred_element_type=jnp.float32
    )
    term_bv = jnp.einsum(
        "tr,tc->rc", value_latent, value_up_gradient, preferred_element_type=jnp.float32
    )
    scale_factor = adapter_scale / math.sqrt(
        token_count * lax.axis_size("seq") * lax.axis_size("dp")
    )
    terms = (term_aq.T, term_bq, term_av.T, term_bv)
    sums = unpacked(summed(packed(terms)), [term.shape for term in terms])
    sum_aq, sum_bq, sum_av, sum_bv = [part * scale_factor for part in sums]
    return (out_rows[None], sum_aq.T, sum_bq, sum_av.T, sum_bv)


def solution(mesh):
    in_specs = (
        P("dp", "seq", None),
        P("dp", "seq", None),
        P("dp", "seq", None),
        P("dp", "seq", None),
        P(),
        P(),
        P(),
        P(),
        P("dp", "seq", None),
    )
    out_specs = (P("dp", "seq", None), P(), P(), P(), P())
    return jax.shard_map(
        on_device, mesh=mesh, in_specs=in_specs, out_specs=out_specs, check_vma=False
    )
```

```python
import functools
import math

import jax
import jax.numpy as jnp
from jax import lax
from jax.experimental import pallas as pl
from jax.experimental.pallas import tpu as pltpu
from jax.sharding import PartitionSpec as P

QUERY_HEADS = 32
KEY_VALUE_HEADS = 4
PER_KEY = 8
WIDTH = 128
RANK = 16
adapter_scale = 2.0
masked_score = -1e30
AXES = ("seq", "dp")
CORE_BIT = 16
PLANE_BITS = (32, 64, 128, 8)
DEPTH_BITS = (1, 2, 4)
CHUNKS = 32
CHUNK_ROWS = 96
NT = (((1,), (1,)), ((), ()))
F32 = jnp.float32
BF16 = jnp.bfloat16
STACK = 4
VMEM_LIMIT = 48 * 1024 * 1024


def groups_of(bits, count):
    groups = []
    for base in range(count):
        if any(base & bit for bit in bits):
            continue
        members = []
        for code in range(1 << len(bits)):
            members.append(base + sum(bit for n, bit in enumerate(bits) if code >> n & 1))
        groups.append(members)
    return groups


def exchanged(value, bits):
    groups = groups_of(bits, lax.axis_size(AXES))
    return lax.all_to_all(value, AXES, 0, 0, axis_index_groups=groups)


def sum_over_first(value):
    return jnp.sum(value.astype(jnp.float32), axis=0)


def spread(value, bits):
    copies = jnp.broadcast_to(value[None], (1 << len(bits),) + value.shape)
    return exchanged(copies, bits)


def swapped(value, bit):
    count = lax.axis_size(AXES)
    return lax.ppermute(value, AXES, [(i, i ^ bit) for i in range(count)])


def shifted(value, axis, by):
    devices = lax.axis_size(axis)
    return lax.ppermute(value, axis, [(i, (i + by) % devices) for i in range(devices)])


def dot_nt(a, b):
    return lax.dot_general(a, b, NT, preferred_element_type=F32)


def dot(a, b):
    return jnp.dot(a, b, preferred_element_type=F32)


def latent_kernel(steps, place_ref, x_ref, dq_ref, dv_ref, k_ref, vf_ref, upv_ref, lat_ref, latt_ref, value_ref, send_ref, acc):
    step = pl.program_id(0)
    down = jnp.concatenate([dq_ref[...], dv_ref[...]], axis=0)
    part = dot_nt(x_ref[...], down)

    @pl.when(step == 0)
    def _():
        acc[...] = part

    @pl.when(step > 0)
    def _():
        acc[...] += part

    @pl.when(step == steps - 1)
    def _():
        whole = acc[...]
        lat = whole.astype(BF16)
        lat_ref[...] = lat
        latt_ref[...] = whole.T.astype(BF16)
        up = dot(lat[:, RANK:], upv_ref[...])
        value_ref[...] = (vf_ref[...].astype(F32) + adapter_scale * up).astype(BF16)
        half = value_ref.shape[1] // 2
        sent = pl.ds(pl.multiple_of(place_ref[0] * half, half), half)
        send_ref[:, :half] = k_ref[:, sent]
        send_ref[:, half:] = value_ref[:, sent]


def latents(place, x, down_q, down_v, keys, value_frozen, up_v, steps=8):
    tokens, model = x.shape
    block = model // steps
    cols = value_frozen.shape[1]
    along = lambda i, s: (0, i)
    whole = lambda i, s: (0, 0)
    return pl.pallas_call(
        functools.partial(latent_kernel, steps),
        grid_spec=pltpu.PrefetchScalarGridSpec(
            num_scalar_prefetch=1,
            grid=(steps,),
            in_specs=[
                pl.BlockSpec((tokens, block), along),
                pl.BlockSpec((RANK, block), along),
                pl.BlockSpec((RANK, block), along),
                pl.BlockSpec((tokens, cols), whole),
                pl.BlockSpec((tokens, cols), whole),
                pl.BlockSpec((RANK, cols), whole),
            ],
            out_specs=[
                pl.BlockSpec((tokens, 2 * RANK), whole),
                pl.BlockSpec((2 * RANK, tokens), whole),
                pl.BlockSpec((tokens, cols), whole),
                pl.BlockSpec((tokens, cols), whole),
            ],
            scratch_shapes=[pltpu.VMEM((tokens, 2 * RANK), F32)],
        ),
        out_shape=[
            jax.ShapeDtypeStruct((tokens, 2 * RANK), BF16),
            jax.ShapeDtypeStruct((2 * RANK, tokens), BF16),
            jax.ShapeDtypeStruct((tokens, cols), BF16),
            jax.ShapeDtypeStruct((tokens, cols), BF16),
        ],
        compiler_params=pltpu.CompilerParams(vmem_limit_bytes=VMEM_LIMIT),
        cost_estimate=pl.CostEstimate(
            flops=2 * tokens * model * 2 * RANK, bytes_accessed=2 * tokens * model, transcendentals=0
        ),
        name="latents",
    )(place, x, down_q, down_v, keys, value_frozen, up_v)


def attend_kernel(far, chained, first_ref, *refs):
    refs = list(refs)
    qf_ref, do_ref, k_ref, v_ref = refs[:4]
    refs = refs[4:]
    if far:
        kp_ref, vp_ref = refs[:2]
        refs = refs[2:]
    lat_ref, latt_ref, upq_ref = refs[:3]
    refs = refs[3:]
    if chained:
        up_in = refs[2]
        refs = refs[3:]
    out_ref, bq_ref, upt_ref, dv_ref = refs[:4]
    refs = refs[4:]
    if far:
        dvp_ref = refs[0]
        refs = refs[1:]
    q_scr, dq_scr = refs

    tokens = qf_ref.shape[0]
    root = 1.0 / math.sqrt(WIDTH)
    base2 = root * math.log2(math.e)
    lat = lat_ref[:, :RANK]
    q_scr[...] = (qf_ref[...].astype(F32) + adapter_scale * dot(lat, upq_ref[...])).astype(BF16)
    if far:
        keys = jnp.concatenate([kp_ref[...], k_ref[...]], axis=0)
        values = jnp.concatenate([vp_ref[...], v_ref[...]], axis=0)
    else:
        keys = k_ref[...]
        values = v_ref[...]
    row = lax.broadcasted_iota(jnp.int32, (STACK * tokens, tokens), 0) % tokens
    col = lax.broadcasted_iota(jnp.int32, (STACK * tokens, tokens), 1)
    seen = col <= row
    dvt = None
    for block in range(PER_KEY // STACK):
        slices = [slice((block * STACK + n) * WIDTH, (block * STACK + n + 1) * WIDTH) for n in range(STACK)]
        q = jnp.concatenate([q_scr[:, cols] for cols in slices], axis=0)
        do = jnp.concatenate([do_ref[:, cols] for cols in slices], axis=0)
        score = dot_nt(q, keys)
        own = jnp.where(seen, score[:, -tokens:], masked_score)
        if far:
            score = jnp.concatenate([score[:, :tokens], own], axis=1)
        else:
            score = own
        top = jnp.max(score, axis=1, keepdims=True)
        expo = jnp.exp2((score - top) * base2)
        prob = expo * (1.0 / jnp.sum(expo, axis=1, keepdims=True))
        prob_b = prob.astype(BF16)
        attended = dot(prob_b, values)
        delta = jnp.sum(do.astype(F32) * attended, axis=1, keepdims=True)
        dprob = dot_nt(do, values)
        dscore = (prob * (dprob - delta)).astype(BF16)
        dq_rows = (dot(dscore, keys) * root).astype(BF16)
        for n, cols in enumerate(slices):
            rows = slice(n * tokens, (n + 1) * tokens)
            out_ref[:, cols] = attended[rows].astype(BF16)
            dq_scr[:, cols] = dq_rows[rows]
        term = lax.dot_general(do, prob_b, (((0,), (0,)), ((), ())), preferred_element_type=F32)
        dvt = term if dvt is None else dvt + term
    dv = dvt.T
    dv_ref[...] = dv[-tokens:]
    if far:
        dvp_ref[...] = dv[:tokens].astype(dvp_ref.dtype)
    dq = dq_scr[...]
    bq_ref[...] = dot(latt_ref[:RANK, :], dq)
    up = dot_nt(upq_ref[...], dq)
    step = pl.program_id(0)

    @pl.when(step == 0)
    def _():
        upt_ref[...] = up + up_in[...] if chained else up

    @pl.when(step > 0)
    def _():
        upt_ref[...] += up


def attend(first, groups, query_frozen, dout, keys, values, prev, lat, latt, up_q, chain):
    tokens = query_frozen.shape[0]
    far = prev is not None
    chained = chain is not None
    wide = PER_KEY * WIDTH
    at_group = lambda i, s: (0, s[0] + i)
    at_step = lambda i, s: (0, i)
    whole = lambda i, s: (0, 0)
    args = [query_frozen, dout, keys, values]
    specs = [
        pl.BlockSpec((tokens, wide), at_group),
        pl.BlockSpec((tokens, wide), at_group),
        pl.BlockSpec((tokens, WIDTH), at_group),
        pl.BlockSpec((tokens, WIDTH), at_group),
    ]
    if far:
        args += [prev, prev]
        specs += [
            pl.BlockSpec((tokens, WIDTH), at_step),
            pl.BlockSpec((tokens, WIDTH), lambda i, s: (0, groups + i)),
        ]
    args += [lat, latt, up_q]
    specs += [
        pl.BlockSpec((tokens, 2 * RANK), whole),
        pl.BlockSpec((2 * RANK, tokens), whole),
        pl.BlockSpec((RANK, wide), at_group),
    ]
    aliases = {}
    if chained:
        aliases = {1 + len(args): 0, 2 + len(args): 1}
        args += list(chain)
        specs += [pl.BlockSpec(memory_space=pl.ANY)] * 2 + [pl.BlockSpec((RANK, tokens), whole)]
    out_specs = [
        pl.BlockSpec((tokens, wide), at_group),
        pl.BlockSpec((RANK, wide), at_group),
        pl.BlockSpec((RANK, tokens), whole),
        pl.BlockSpec((tokens, WIDTH), at_step),
    ]
    out_shape = [
        jax.ShapeDtypeStruct(query_frozen.shape, BF16),
        jax.ShapeDtypeStruct(up_q.shape, F32),
        jax.ShapeDtypeStruct((RANK, tokens), F32),
        jax.ShapeDtypeStruct((tokens, groups * WIDTH), F32),
    ]
    if far:
        out_specs.append(pl.BlockSpec((tokens, WIDTH), at_step))
        out_shape.append(jax.ShapeDtypeStruct((tokens, groups * WIDTH), BF16))
    span = tokens * (2 if far else 1)
    return pl.pallas_call(
        functools.partial(attend_kernel, far, chained),
        grid_spec=pltpu.PrefetchScalarGridSpec(
            num_scalar_prefetch=1,
            grid=(groups,),
            in_specs=specs,
            out_specs=out_specs,
            scratch_shapes=[pltpu.VMEM((tokens, wide), BF16), pltpu.VMEM((tokens, wide), BF16)],
        ),
        out_shape=out_shape,
        input_output_aliases=aliases,
        compiler_params=pltpu.CompilerParams(vmem_limit_bytes=VMEM_LIMIT),
        cost_estimate=pl.CostEstimate(
            flops=groups * 10 * tokens * span * wide,
            bytes_accessed=groups * 6 * tokens * wide,
            transcendentals=groups * PER_KEY * tokens * span,
        ),
        name="attend_far" if far else "attend_near",
    )(first, *args)


def outer_kernel(fresh, half_ref, *refs):
    refs = list(refs)
    x_ref, bq_ref, latt_ref, dv_ref = refs[:4]
    refs = refs[4:]
    if fresh:
        upt_ref, near_ref, back_ref, upv_far, upv_near, out_ref, both_ref, near_out, bv_scr = refs
    else:
        both_ref, out_ref, bv_scr = refs
    step = pl.program_id(0)

    @pl.when(step == 0)
    def _():
        dvb = dv_ref[...].astype(BF16)
        bv_scr[...] = dot(latt_ref[RANK:, :], dvb)
        if fresh:
            near = (near_ref[...] + back_ref[...].astype(F32)).astype(BF16)
            near_out[...] = near
            upv = dot_nt(upv_far[...], dvb) + dot_nt(upv_near[...], near)
            both_ref[...] = jnp.concatenate([upt_ref[...], upv], axis=0).astype(BF16)

    part = dot(both_ref[...], x_ref[...])
    for chunk in range(out_ref.shape[0]):
        for lane in range(2):
            cols = slice((2 * chunk + lane) * WIDTH, (2 * chunk + lane + 1) * WIDTH)
            rows = slice(lane * RANK, (lane + 1) * RANK)
            out_ref[chunk, rows, :] = part[:RANK, cols].astype(out_ref.dtype)
            rows = slice((2 + lane) * RANK, (3 + lane) * RANK)
            out_ref[chunk, rows, :] = part[RANK:, cols].astype(out_ref.dtype)
        cols = slice(chunk * WIDTH, (chunk + 1) * WIDTH)
        out_ref[chunk, 4 * RANK : 5 * RANK, :] = bq_ref[:, cols].astype(out_ref.dtype)
        out_ref[chunk, 5 * RANK :, :] = jnp.zeros((RANK, WIDTH), out_ref.dtype)

    @pl.when(step == 0)
    def _():
        for chunk in range(2):
            cols = slice(chunk * WIDTH, (chunk + 1) * WIDTH)
            out_ref[chunk, 5 * RANK :, :] = bv_scr[:, cols].astype(out_ref.dtype)


def outer(half, x, bq, latt, dv, dtype, fresh=None, both=None, steps=4):
    tokens, model = x.shape
    per_step = CHUNKS // 2 // steps
    along = lambda i, s: (0, s[0] * steps + i)
    whole = lambda i, s: (0, 0)
    cols = dv.shape[1]
    args = [x, bq, latt, dv]
    specs = [
        pl.BlockSpec((tokens, per_step * 2 * WIDTH), along),
        pl.BlockSpec((RANK, per_step * WIDTH), along),
        pl.BlockSpec((2 * RANK, tokens), whole),
        pl.BlockSpec((tokens, cols), whole),
    ]
    out_specs = [pl.BlockSpec((per_step, CHUNK_ROWS, WIDTH), lambda i, s: (i, 0, 0))]
    out_shape = [jax.ShapeDtypeStruct((CHUNKS // 2, CHUNK_ROWS, WIDTH), dtype)]
    if fresh is not None:
        upt, near, back, up_v = fresh
        args += [upt, near, back, up_v, up_v]
        specs += [
            pl.BlockSpec((RANK, tokens), whole),
            pl.BlockSpec((tokens, cols), whole),
            pl.BlockSpec((tokens, cols), whole),
            pl.BlockSpec((RANK, cols), lambda i, s: (0, s[0])),
            pl.BlockSpec((RANK, cols), lambda i, s: (0, 1 - s[0])),
        ]
        out_specs += [pl.BlockSpec((2 * RANK, tokens), whole), pl.BlockSpec((tokens, cols), whole)]
        out_shape += [
            jax.ShapeDtypeStruct((2 * RANK, tokens), BF16),
            jax.ShapeDtypeStruct((tokens, cols), BF16),
        ]
    else:
        args.append(both)
        specs.append(pl.BlockSpec((2 * RANK, tokens), whole))
    return pl.pallas_call(
        functools.partial(outer_kernel, fresh is not None),
        grid_spec=pltpu.PrefetchScalarGridSpec(
            num_scalar_prefetch=1,
            grid=(steps,),
            in_specs=specs,
            out_specs=out_specs,
            scratch_shapes=[pltpu.VMEM((RANK, cols), F32)],
        ),
        out_shape=out_shape,
        compiler_params=pltpu.CompilerParams(vmem_limit_bytes=VMEM_LIMIT),
        cost_estimate=pl.CostEstimate(
            flops=2 * tokens * model * RANK, bytes_accessed=tokens * model, transcendentals=0
        ),
        name="outer_first" if fresh is not None else "outer_second",
    )(half, *args)


def unpack_kernel(scale, half_ref, own_ref, other_ref, aq_ref, av_ref, bq_ref, bv_ref):
    def fill(ref):
        for chunk in range(CHUNKS // 2):
            for lane in range(2):
                cols = slice((2 * chunk + lane) * WIDTH, (2 * chunk + lane + 1) * WIDTH)
                rows = slice(lane * RANK, (lane + 1) * RANK)
                aq_ref[:, cols] = ref[chunk, rows, :].astype(F32) * scale
                rows = slice((2 + lane) * RANK, (3 + lane) * RANK)
                av_ref[:, cols] = ref[chunk, rows, :].astype(F32) * scale
            cols = slice(chunk * WIDTH, (chunk + 1) * WIDTH)
            bq_ref[:, cols] = ref[chunk, 4 * RANK : 5 * RANK, :].astype(F32) * scale
            if chunk < 2:
                bv_ref[:, cols] = ref[chunk, 5 * RANK :, :].astype(F32) * scale

    @pl.when(pl.program_id(0) == 0)
    def _():
        fill(own_ref)

    @pl.when(pl.program_id(0) == 1)
    def _():
        fill(other_ref)


def unpacked(half, own, other, scale, shapes):
    flip = lambda i, s: (0, (s[0] + i) % 2)
    whole = lambda i, s: (0, 0, 0)
    return pl.pallas_call(
        functools.partial(unpack_kernel, scale),
        grid_spec=pltpu.PrefetchScalarGridSpec(
            num_scalar_prefetch=1,
            grid=(2,),
            in_specs=[pl.BlockSpec(own.shape, whole)] * 2,
            out_specs=[pl.BlockSpec((rows, cols // 2), flip) for rows, cols in shapes],
        ),
        out_shape=[jax.ShapeDtypeStruct(shape, F32) for shape in shapes],
        compiler_params=pltpu.CompilerParams(vmem_limit_bytes=VMEM_LIMIT),
        cost_estimate=pl.CostEstimate(flops=0, bytes_accessed=3 * 1024 * 1024, transcendentals=0),
        name="unpack",
    )(half, own, other)


def summed(given, kept):
    halves = kept + swapped(given, CORE_BIT).astype(F32)
    piece = sum_over_first(exchanged(halves.astype(BF16), PLANE_BITS))
    piece = sum_over_first(spread(piece.astype(BF16), DEPTH_BITS))
    return spread(piece.astype(BF16), PLANE_BITS)


def on_device(
    normed,
    query_frozen,
    key_projected,
    value_frozen,
    query_down_weight,
    query_up_weight,
    value_down_weight,
    value_up_weight,
    output_cotangent,
):
    x, qf, keys, vf, dout = [
        a[0] for a in (normed, query_frozen, key_projected, value_frozen, output_cotangent)
    ]
    tokens = x.shape[0]
    parity = lax.axis_index("seq") % 2
    place = parity.reshape(1).astype(jnp.int32)
    away = 1 - place
    pair = KEY_VALUE_HEADS // 2
    lat, latt, values, sent = latents(
        place, x, query_down_weight.T, value_down_weight.T, keys, vf, value_up_weight
    )
    prev = shifted(sent, "seq", 1)
    out, bq, upt, dv_near = attend(
        pair * place, pair, qf, dout, keys, values, None, lat, latt, query_up_weight, None
    )
    out, bq, upt, dv_far, dv_back = attend(
        pair * away, pair, qf, dout, keys, values, prev, lat, latt, query_up_weight, (out, bq, upt)
    )
    back = shifted(dv_back, "seq", -1)
    given, both, near = outer(
        away, x, bq, latt, dv_far, BF16, fresh=(upt, dv_near, back, value_up_weight)
    )
    (kept,) = outer(place, x, bq, latt, near, F32, both=both)
    own_half = summed(given, kept)
    other_half = swapped(own_half, CORE_BIT)
    scale_factor = adapter_scale / math.sqrt(tokens * lax.axis_size("seq") * lax.axis_size("dp"))
    model = x.shape[1]
    shapes = [(RANK, model), (RANK, model), (RANK, qf.shape[1]), (RANK, vf.shape[1])]
    aq, av, bq_sum, bv_sum = unpacked(place, own_half, other_half, scale_factor, shapes)
    return (out[None], aq.T, bq_sum, av.T, bv_sum)


def solution(mesh):
    in_specs = (
        P("dp", "seq", None),
        P("dp", "seq", None),
        P("dp", "seq", None),
        P("dp", "seq", None),
        P(),
        P(),
        P(),
        P(),
        P("dp", "seq", None),
    )
    out_specs = (P("dp", "seq", None), P(), P(), P(), P())
    return jax.shard_map(
        on_device, mesh=mesh, in_specs=in_specs, out_specs=out_specs, check_vma=False
    )
```

```python
import functools
import math

import jax
import jax.numpy as jnp
from jax import lax
from jax.experimental import pallas as pl
from jax.experimental.pallas import tpu as pltpu
from jax.sharding import PartitionSpec as P

QUERY_HEADS = 32
KEY_VALUE_HEADS = 4
PER_KEY = 8
WIDTH = 128
RANK = 16
adapter_scale = 2.0
masked_score = -1e30
AXES = ("seq", "dp")
CORE_BIT = 16
PLANE_BITS = (32, 64, 128, 8)
DEPTH_STEPS = (1, 2, 7)
CHUNKS = 32
CHUNK_ROWS = 96
NT = (((1,), (1,)), ((), ()))
F32 = jnp.float32
BF16 = jnp.bfloat16
STACK = 4
VMEM_LIMIT = 48 * 1024 * 1024


def groups_of(bits, count):
    groups = []
    for base in range(count):
        if any(base & bit for bit in bits):
            continue
        members = []
        for code in range(1 << len(bits)):
            members.append(base + sum(bit for n, bit in enumerate(bits) if code >> n & 1))
        groups.append(members)
    return groups


def exchanged(value, bits):
    groups = groups_of(bits, lax.axis_size(AXES))
    return lax.all_to_all(value, AXES, 0, 0, axis_index_groups=groups)


def sum_over_first(value):
    return jnp.sum(value.astype(jnp.float32), axis=0)


def spread(value, bits):
    copies = jnp.broadcast_to(value[None], (1 << len(bits),) + value.shape)
    return exchanged(copies, bits)


def swapped(value, bit):
    count = lax.axis_size(AXES)
    return lax.ppermute(value, AXES, [(i, i ^ bit) for i in range(count)])


def shifted(value, axis, by):
    devices = lax.axis_size(axis)
    return lax.ppermute(value, axis, [(i, (i + by) % devices) for i in range(devices)])


def dot_nt(a, b):
    return lax.dot_general(a, b, NT, preferred_element_type=F32)


def dot(a, b):
    return jnp.dot(a, b, preferred_element_type=F32)


def in_hbm(value):
    return pltpu.with_memory_space_constraint(value, pltpu.HBM)


def latent_kernel(steps, place_ref, x_hbm, dq_hbm, dv_hbm, vf_hbm, upv_hbm, lat_ref, latt_ref, value_ref, send_ref, x_buf, down, vf_buf, up_buf, sems):
    tokens, model = x_buf.shape
    block = model // steps
    first = [
        pltpu.make_async_copy(dq_hbm, down.at[pl.ds(0, RANK)], sems.at[steps]),
        pltpu.make_async_copy(dv_hbm, down.at[pl.ds(RANK, RANK)], sems.at[steps + 1]),
    ]
    last = [
        pltpu.make_async_copy(vf_hbm, vf_buf, sems.at[steps + 2]),
        pltpu.make_async_copy(upv_hbm, up_buf, sems.at[steps + 3]),
    ]
    pieces = []
    for step in range(steps):
        cols = pl.ds(step * block, block)
        pieces.append(pltpu.make_async_copy(x_hbm.at[:, cols], x_buf.at[:, cols], sems.at[step]))
    for copy in first + pieces + last:
        copy.start()
    for copy in first:
        copy.wait()
    whole = None
    for step in range(steps):
        pieces[step].wait()
        cols = slice(step * block, (step + 1) * block)
        part = dot_nt(x_buf[:, cols], down[:, cols])
        whole = part if whole is None else whole + part
    for copy in last:
        copy.wait()
    lat = whole.astype(BF16)
    lat_ref[...] = lat
    latt_ref[...] = whole.T.astype(BF16)
    up = dot(lat[:, RANK:], up_buf[...])
    value_ref[...] = (vf_buf[...].astype(F32) + adapter_scale * up).astype(BF16)
    half = value_ref.shape[1] // 2
    send_ref[...] = value_ref[:, pl.ds(pl.multiple_of(place_ref[0] * half, half), half)]


def latents(place, x, down_q, down_v, value_frozen, up_v, steps=8):
    tokens, model = x.shape
    cols = value_frozen.shape[1]
    whole = lambda i, s: (0, 0)
    return pl.pallas_call(
        functools.partial(latent_kernel, steps),
        grid_spec=pltpu.PrefetchScalarGridSpec(
            num_scalar_prefetch=1,
            grid=(1,),
            in_specs=[pl.BlockSpec(memory_space=pl.ANY)] * 5,
            out_specs=[
                pl.BlockSpec((tokens, 2 * RANK), whole),
                pl.BlockSpec((2 * RANK, tokens), whole),
                pl.BlockSpec((tokens, cols), whole),
                pl.BlockSpec((tokens, cols // 2), whole),
            ],
            scratch_shapes=[
                pltpu.VMEM((tokens, model), BF16),
                pltpu.VMEM((2 * RANK, model), BF16),
                pltpu.VMEM((tokens, cols), BF16),
                pltpu.VMEM((RANK, cols), BF16),
                pltpu.SemaphoreType.DMA((steps + 4,)),
            ],
        ),
        out_shape=[
            jax.ShapeDtypeStruct((tokens, 2 * RANK), BF16),
            jax.ShapeDtypeStruct((2 * RANK, tokens), BF16),
            jax.ShapeDtypeStruct((tokens, cols), BF16),
            jax.ShapeDtypeStruct((tokens, cols // 2), BF16),
        ],
        compiler_params=pltpu.CompilerParams(vmem_limit_bytes=48 * 1024 * 1024),
        cost_estimate=pl.CostEstimate(
            flops=2 * tokens * model * 2 * RANK, bytes_accessed=2 * tokens * model, transcendentals=0
        ),
        name="latents",
    )(place, *[in_hbm(a) for a in (x, down_q, down_v, value_frozen, up_v)])


def attend_kernel(far, chained, first_ref, *refs):
    refs = list(refs)
    qf_ref, do_ref, k_ref, v_ref = refs[:4]
    refs = refs[4:]
    if far:
        kp_ref, vp_ref = refs[:2]
        refs = refs[2:]
    lat_ref, latt_ref, upq_ref = refs[:3]
    refs = refs[3:]
    if chained:
        up_in = refs[2]
        refs = refs[3:]
    out_ref, bq_ref, upt_ref, dv_ref = refs[:4]
    refs = refs[4:]
    if far:
        dvp_ref = refs[0]
        refs = refs[1:]
    q_scr, dq_scr = refs

    tokens = qf_ref.shape[0]
    root = 1.0 / math.sqrt(WIDTH)
    base2 = root * math.log2(math.e)
    lat = lat_ref[:, :RANK]
    q_scr[...] = (qf_ref[...].astype(F32) + adapter_scale * dot(lat, upq_ref[...])).astype(BF16)
    if far:
        keys = jnp.concatenate([kp_ref[...], k_ref[...]], axis=0)
        values = jnp.concatenate([vp_ref[...], v_ref[...]], axis=0)
    else:
        keys = k_ref[...]
        values = v_ref[...]
    row = lax.broadcasted_iota(jnp.int32, (STACK * tokens, tokens), 0) % tokens
    col = lax.broadcasted_iota(jnp.int32, (STACK * tokens, tokens), 1)
    seen = col <= row
    dvt = None
    for block in range(PER_KEY // STACK):
        slices = [slice((block * STACK + n) * WIDTH, (block * STACK + n + 1) * WIDTH) for n in range(STACK)]
        q = jnp.concatenate([q_scr[:, cols] for cols in slices], axis=0)
        do = jnp.concatenate([do_ref[:, cols] for cols in slices], axis=0)
        score = dot_nt(q, keys)
        own = jnp.where(seen, score[:, -tokens:], masked_score)
        if far:
            score = jnp.concatenate([score[:, :tokens], own], axis=1)
        else:
            score = own
        top = jnp.max(score, axis=1, keepdims=True)
        expo = jnp.exp2((score - top) * base2)
        prob = expo * (1.0 / jnp.sum(expo, axis=1, keepdims=True))
        prob_b = prob.astype(BF16)
        attended = dot(prob_b, values)
        delta = jnp.sum(do.astype(F32) * attended, axis=1, keepdims=True)
        dprob = dot_nt(do, values)
        dscore = (prob * (dprob - delta)).astype(BF16)
        dq_rows = (dot(dscore, keys) * root).astype(BF16)
        for n, cols in enumerate(slices):
            rows = slice(n * tokens, (n + 1) * tokens)
            out_ref[:, cols] = attended[rows].astype(BF16)
            dq_scr[:, cols] = dq_rows[rows]
        term = lax.dot_general(do, prob_b, (((0,), (0,)), ((), ())), preferred_element_type=F32)
        dvt = term if dvt is None else dvt + term
    dv = dvt.T
    dv_ref[...] = dv[-tokens:]
    if far:
        dvp_ref[...] = dv[:tokens].astype(dvp_ref.dtype)
    dq = dq_scr[...]
    bq_ref[...] = dot(latt_ref[:RANK, :], dq)
    up = dot_nt(upq_ref[...], dq)
    step = pl.program_id(0)

    @pl.when(step == 0)
    def _():
        upt_ref[...] = up + up_in[...] if chained else up

    @pl.when(step > 0)
    def _():
        upt_ref[...] += up


def attend(first, groups, query_frozen, dout, keys, values, prev, lat, latt, up_q, chain):
    tokens = query_frozen.shape[0]
    far = prev is not None
    chained = chain is not None
    wide = PER_KEY * WIDTH
    at_group = lambda i, s: (0, s[0] + i)
    at_step = lambda i, s: (0, i)
    whole = lambda i, s: (0, 0)
    args = [query_frozen, dout, keys, values]
    specs = [
        pl.BlockSpec((tokens, wide), at_group),
        pl.BlockSpec((tokens, wide), at_group),
        pl.BlockSpec((tokens, WIDTH), at_group),
        pl.BlockSpec((tokens, WIDTH), at_group),
    ]
    if far:
        args += list(prev)
        specs += [pl.BlockSpec((tokens, WIDTH), at_group), pl.BlockSpec((tokens, WIDTH), at_step)]
    args += [lat, latt, up_q]
    specs += [
        pl.BlockSpec((tokens, 2 * RANK), whole),
        pl.BlockSpec((2 * RANK, tokens), whole),
        pl.BlockSpec((RANK, wide), at_group),
    ]
    aliases = {}
    if chained:
        aliases = {1 + len(args): 0, 2 + len(args): 1}
        args += list(chain)
        specs += [pl.BlockSpec(memory_space=pl.ANY)] * 2 + [pl.BlockSpec((RANK, tokens), whole)]
    out_specs = [
        pl.BlockSpec((tokens, wide), at_group),
        pl.BlockSpec((RANK, wide), at_group),
        pl.BlockSpec((RANK, tokens), whole),
        pl.BlockSpec((tokens, WIDTH), at_step),
    ]
    out_shape = [
        jax.ShapeDtypeStruct(query_frozen.shape, BF16),
        jax.ShapeDtypeStruct(up_q.shape, F32),
        jax.ShapeDtypeStruct((RANK, tokens), F32),
        jax.ShapeDtypeStruct((tokens, groups * WIDTH), F32),
    ]
    if far:
        out_specs.append(pl.BlockSpec((tokens, WIDTH), at_step))
        out_shape.append(jax.ShapeDtypeStruct((tokens, groups * WIDTH), BF16))
    span = tokens * (2 if far else 1)
    return pl.pallas_call(
        functools.partial(attend_kernel, far, chained),
        grid_spec=pltpu.PrefetchScalarGridSpec(
            num_scalar_prefetch=1,
            grid=(groups,),
            in_specs=specs,
            out_specs=out_specs,
            scratch_shapes=[pltpu.VMEM((tokens, wide), BF16), pltpu.VMEM((tokens, wide), BF16)],
        ),
        out_shape=out_shape,
        input_output_aliases=aliases,
        compiler_params=pltpu.CompilerParams(vmem_limit_bytes=VMEM_LIMIT),
        cost_estimate=pl.CostEstimate(
            flops=groups * 10 * tokens * span * wide,
            bytes_accessed=groups * 6 * tokens * wide,
            transcendentals=groups * PER_KEY * tokens * span,
        ),
        name="attend_far" if far else "attend_near",
    )(first, *args)


def outer_kernel(fresh, half_ref, *refs):
    refs = list(refs)
    x_ref, bq_ref, latt_ref, dv_ref = refs[:4]
    refs = refs[4:]
    if fresh:
        upt_ref, near_ref, back_ref, upv_far, upv_near, out_ref, both_ref, near_out, bv_scr = refs
    else:
        both_ref, out_ref, bv_scr = refs
    step = pl.program_id(0)

    @pl.when(step == 0)
    def _():
        dvb = dv_ref[...].astype(BF16)
        bv_scr[...] = dot(latt_ref[RANK:, :], dvb)
        if fresh:
            near = (near_ref[...] + back_ref[...].astype(F32)).astype(BF16)
            near_out[...] = near
            upv = dot_nt(upv_far[...], dvb) + dot_nt(upv_near[...], near)
            both_ref[...] = jnp.concatenate([upt_ref[...], upv], axis=0).astype(BF16)

    part = dot(both_ref[...], x_ref[...])
    for chunk in range(out_ref.shape[0]):
        for lane in range(2):
            cols = slice((2 * chunk + lane) * WIDTH, (2 * chunk + lane + 1) * WIDTH)
            rows = slice(lane * RANK, (lane + 1) * RANK)
            out_ref[chunk, rows, :] = part[:RANK, cols].astype(out_ref.dtype)
            rows = slice((2 + lane) * RANK, (3 + lane) * RANK)
            out_ref[chunk, rows, :] = part[RANK:, cols].astype(out_ref.dtype)
        cols = slice(chunk * WIDTH, (chunk + 1) * WIDTH)
        out_ref[chunk, 4 * RANK : 5 * RANK, :] = bq_ref[:, cols].astype(out_ref.dtype)
        out_ref[chunk, 5 * RANK :, :] = jnp.zeros((RANK, WIDTH), out_ref.dtype)

    @pl.when(step == 0)
    def _():
        for chunk in range(2):
            cols = slice(chunk * WIDTH, (chunk + 1) * WIDTH)
            out_ref[chunk, 5 * RANK :, :] = bv_scr[:, cols].astype(out_ref.dtype)


def outer(half, x, bq, latt, dv, dtype, fresh=None, both=None, steps=4):
    tokens, model = x.shape
    per_step = CHUNKS // 2 // steps
    along = lambda i, s: (0, s[0] * steps + i)
    whole = lambda i, s: (0, 0)
    cols = dv.shape[1]
    args = [x, bq, latt, dv]
    specs = [
        pl.BlockSpec((tokens, per_step * 2 * WIDTH), along),
        pl.BlockSpec((RANK, per_step * WIDTH), along),
        pl.BlockSpec((2 * RANK, tokens), whole),
        pl.BlockSpec((tokens, cols), whole),
    ]
    out_specs = [pl.BlockSpec((per_step, CHUNK_ROWS, WIDTH), lambda i, s: (i, 0, 0))]
    out_shape = [jax.ShapeDtypeStruct((CHUNKS // 2, CHUNK_ROWS, WIDTH), dtype)]
    if fresh is not None:
        upt, near, back, up_v = fresh
        args += [upt, near, back, up_v, up_v]
        specs += [
            pl.BlockSpec((RANK, tokens), whole),
            pl.BlockSpec((tokens, cols), whole),
            pl.BlockSpec((tokens, cols), whole),
            pl.BlockSpec((RANK, cols), lambda i, s: (0, s[0])),
            pl.BlockSpec((RANK, cols), lambda i, s: (0, 1 - s[0])),
        ]
        out_specs += [pl.BlockSpec((2 * RANK, tokens), whole), pl.BlockSpec((tokens, cols), whole)]
        out_shape += [
            jax.ShapeDtypeStruct((2 * RANK, tokens), BF16),
            jax.ShapeDtypeStruct((tokens, cols), BF16),
        ]
    else:
        args.append(both)
        specs.append(pl.BlockSpec((2 * RANK, tokens), whole))
    return pl.pallas_call(
        functools.partial(outer_kernel, fresh is not None),
        grid_spec=pltpu.PrefetchScalarGridSpec(
            num_scalar_prefetch=1,
            grid=(steps,),
            in_specs=specs,
            out_specs=out_specs,
            scratch_shapes=[pltpu.VMEM((RANK, cols), F32)],
        ),
        out_shape=out_shape,
        compiler_params=pltpu.CompilerParams(vmem_limit_bytes=VMEM_LIMIT),
        cost_estimate=pl.CostEstimate(
            flops=2 * tokens * model * RANK, bytes_accessed=tokens * model, transcendentals=0
        ),
        name="outer_first" if fresh is not None else "outer_second",
    )(half, *args)


def unpack_kernel(scale, half_ref, own_ref, other_ref, aq_ref, av_ref, bq_ref, bv_ref):
    def fill(ref):
        for chunk in range(CHUNKS // 2):
            for lane in range(2):
                cols = slice((2 * chunk + lane) * WIDTH, (2 * chunk + lane + 1) * WIDTH)
                rows = slice(lane * RANK, (lane + 1) * RANK)
                aq_ref[:, cols] = ref[chunk, rows, :].astype(F32) * scale
                rows = slice((2 + lane) * RANK, (3 + lane) * RANK)
                av_ref[:, cols] = ref[chunk, rows, :].astype(F32) * scale
            cols = slice(chunk * WIDTH, (chunk + 1) * WIDTH)
            bq_ref[:, cols] = ref[chunk, 4 * RANK : 5 * RANK, :].astype(F32) * scale
            if chunk < 2:
                bv_ref[:, cols] = ref[chunk, 5 * RANK :, :].astype(F32) * scale

    @pl.when(pl.program_id(0) == 0)
    def _():
        fill(own_ref)

    @pl.when(pl.program_id(0) == 1)
    def _():
        fill(other_ref)


def unpacked(half, own, other, scale, shapes):
    flip = lambda i, s: (0, (s[0] + i) % 2)
    whole = lambda i, s: (0, 0, 0)
    return pl.pallas_call(
        functools.partial(unpack_kernel, scale),
        grid_spec=pltpu.PrefetchScalarGridSpec(
            num_scalar_prefetch=1,
            grid=(2,),
            in_specs=[pl.BlockSpec(own.shape, whole)] * 2,
            out_specs=[pl.BlockSpec((rows, cols // 2), flip) for rows, cols in shapes],
        ),
        out_shape=[jax.ShapeDtypeStruct(shape, F32) for shape in shapes],
        compiler_params=pltpu.CompilerParams(vmem_limit_bytes=VMEM_LIMIT),
        cost_estimate=pl.CostEstimate(flops=0, bytes_accessed=3 * 1024 * 1024, transcendentals=0),
        name="unpack",
    )(half, own, other)


def summed(given, kept):
    halves = kept + swapped(given, CORE_BIT).astype(F32)
    piece = sum_over_first(exchanged(halves.astype(BF16), PLANE_BITS))
    for bits in DEPTH_STEPS:
        mine = piece.astype(BF16)
        piece = mine.astype(F32) + swapped(mine, bits).astype(F32)
    return spread(piece.astype(BF16), PLANE_BITS)


def on_device(
    normed,
    query_frozen,
    key_projected,
    value_frozen,
    query_down_weight,
    query_up_weight,
    value_down_weight,
    value_up_weight,
    output_cotangent,
):
    x, qf, keys, vf, dout = [
        a[0] for a in (normed, query_frozen, key_projected, value_frozen, output_cotangent)
    ]
    tokens = x.shape[0]
    parity = lax.axis_index("seq") % 2
    place = parity.reshape(1).astype(jnp.int32)
    away = 1 - place
    pair = KEY_VALUE_HEADS // 2
    prev_keys = shifted(keys, "seq", 1)
    lat, latt, values, sent = latents(
        place, x, query_down_weight.T, value_down_weight.T, vf, value_up_weight
    )
    prev = (prev_keys, shifted(sent, "seq", 1))
    out, bq, upt, dv_near = attend(
        pair * place, pair, qf, dout, keys, values, None, lat, latt, query_up_weight, None
    )
    out, bq, upt, dv_far, dv_back = attend(
        pair * away, pair, qf, dout, keys, values, prev, lat, latt, query_up_weight, (out, bq, upt)
    )
    back = shifted(dv_back, "seq", -1)
    given, both, near = outer(
        away, x, bq, latt, dv_far, BF16, fresh=(upt, dv_near, back, value_up_weight)
    )
    (kept,) = outer(place, x, bq, latt, near, F32, both=both)
    own_half = summed(given, kept)
    other_half = swapped(own_half, CORE_BIT)
    scale_factor = adapter_scale / math.sqrt(tokens * lax.axis_size("seq") * lax.axis_size("dp"))
    model = x.shape[1]
    shapes = [(RANK, model), (RANK, model), (RANK, qf.shape[1]), (RANK, vf.shape[1])]
    aq, av, bq_sum, bv_sum = unpacked(place, own_half, other_half, scale_factor, shapes)
    return (out[None], aq.T, bq_sum, av.T, bv_sum)


def solution(mesh):
    in_specs = (
        P("dp", "seq", None),
        P("dp", "seq", None),
        P("dp", "seq", None),
        P("dp", "seq", None),
        P(),
        P(),
        P(),
        P(),
        P("dp", "seq", None),
    )
    out_specs = (P("dp", "seq", None), P(), P(), P(), P())
    return jax.shard_map(
        on_device, mesh=mesh, in_specs=in_specs, out_specs=out_specs, check_vma=False
    )
```

```python
import functools
import math

import jax
import jax.numpy as jnp
from jax import lax
from jax.experimental import pallas as pl
from jax.experimental.pallas import tpu as pltpu
from jax.sharding import PartitionSpec as P

QUERY_HEADS = 32
KEY_VALUE_HEADS = 4
PER_KEY = 8
WIDTH = 128
RANK = 16
adapter_scale = 2.0
masked_score = -1e30
AXES = ("seq", "dp")
CORE_BIT = 16
PLANE_BITS = (128, 8, 32, 64)
DEPTH_STEPS = (1, 2, 7)
CHUNKS = 32
CHUNK_ROWS = 96
NT = (((1,), (1,)), ((), ()))
F32 = jnp.float32
BF16 = jnp.bfloat16
STACK = 4
VMEM_LIMIT = 48 * 1024 * 1024


def groups_of(bits, count):
    groups = []
    for base in range(count):
        if any(base & bit for bit in bits):
            continue
        members = []
        for code in range(1 << len(bits)):
            members.append(base + sum(bit for n, bit in enumerate(bits) if code >> n & 1))
        groups.append(members)
    return groups


def exchanged(value, bits):
    groups = groups_of(bits, lax.axis_size(AXES))
    return lax.all_to_all(value, AXES, 0, 0, axis_index_groups=groups)


def sum_over_first(value):
    return jnp.sum(value.astype(jnp.float32), axis=0)


def spread(value, bits):
    copies = jnp.broadcast_to(value[None], (1 << len(bits),) + value.shape)
    return exchanged(copies, bits)


def swapped(value, bit):
    count = lax.axis_size(AXES)
    return lax.ppermute(value, AXES, [(i, i ^ bit) for i in range(count)])


def shifted(value, axis, by):
    devices = lax.axis_size(axis)
    return lax.ppermute(value, axis, [(i, (i + by) % devices) for i in range(devices)])


def dot_nt(a, b):
    return lax.dot_general(a, b, NT, preferred_element_type=F32)


def dot(a, b):
    return jnp.dot(a, b, preferred_element_type=F32)


def in_hbm(value):
    return pltpu.with_memory_space_constraint(value, pltpu.HBM)


def latent_kernel(steps, place_ref, x_hbm, dq_hbm, dv_hbm, vf_hbm, upv_hbm, lat_ref, latt_ref, value_ref, send_ref, x_buf, down, vf_buf, up_buf, sems):
    tokens, model = x_buf.shape
    block = model // steps
    first = [
        pltpu.make_async_copy(dq_hbm, down.at[pl.ds(0, RANK)], sems.at[steps]),
        pltpu.make_async_copy(dv_hbm, down.at[pl.ds(RANK, RANK)], sems.at[steps + 1]),
    ]
    last = [
        pltpu.make_async_copy(vf_hbm, vf_buf, sems.at[steps + 2]),
        pltpu.make_async_copy(upv_hbm, up_buf, sems.at[steps + 3]),
    ]
    pieces = []
    for step in range(steps):
        cols = pl.ds(step * block, block)
        pieces.append(pltpu.make_async_copy(x_hbm.at[:, cols], x_buf.at[:, cols], sems.at[step]))
    for copy in first + pieces + last:
        copy.start()
    for copy in first:
        copy.wait()
    whole = None
    for step in range(steps):
        pieces[step].wait()
        cols = slice(step * block, (step + 1) * block)
        part = dot_nt(x_buf[:, cols], down[:, cols])
        whole = part if whole is None else whole + part
    for copy in last:
        copy.wait()
    lat = whole.astype(BF16)
    lat_ref[...] = lat
    latt_ref[...] = whole.T.astype(BF16)
    up = dot(lat[:, RANK:], up_buf[...])
    value_ref[...] = (vf_buf[...].astype(F32) + adapter_scale * up).astype(BF16)
    half = value_ref.shape[1] // 2
    send_ref[...] = value_ref[:, pl.ds(pl.multiple_of(place_ref[0] * half, half), half)]


def latents(place, x, down_q, down_v, value_frozen, up_v, steps=8):
    tokens, model = x.shape
    cols = value_frozen.shape[1]
    whole = lambda i, s: (0, 0)
    return pl.pallas_call(
        functools.partial(latent_kernel, steps),
        grid_spec=pltpu.PrefetchScalarGridSpec(
            num_scalar_prefetch=1,
            grid=(1,),
            in_specs=[pl.BlockSpec(memory_space=pl.ANY)] * 5,
            out_specs=[
                pl.BlockSpec((tokens, 2 * RANK), whole),
                pl.BlockSpec((2 * RANK, tokens), whole),
                pl.BlockSpec((tokens, cols), whole),
                pl.BlockSpec((tokens, cols // 2), whole),
            ],
            scratch_shapes=[
                pltpu.VMEM((tokens, model), BF16),
                pltpu.VMEM((2 * RANK, model), BF16),
                pltpu.VMEM((tokens, cols), BF16),
                pltpu.VMEM((RANK, cols), BF16),
                pltpu.SemaphoreType.DMA((steps + 4,)),
            ],
        ),
        out_shape=[
            jax.ShapeDtypeStruct((tokens, 2 * RANK), BF16),
            jax.ShapeDtypeStruct((2 * RANK, tokens), BF16),
            jax.ShapeDtypeStruct((tokens, cols), BF16),
            jax.ShapeDtypeStruct((tokens, cols // 2), BF16),
        ],
        compiler_params=pltpu.CompilerParams(vmem_limit_bytes=48 * 1024 * 1024),
        cost_estimate=pl.CostEstimate(
            flops=2 * tokens * model * 2 * RANK, bytes_accessed=2 * tokens * model, transcendentals=0
        ),
        name="latents",
    )(place, *[in_hbm(a) for a in (x, down_q, down_v, value_frozen, up_v)])


def attend_kernel(far, chained, first_ref, *refs):
    refs = list(refs)
    qf_ref, do_ref, k_ref, v_ref = refs[:4]
    refs = refs[4:]
    if far:
        kp_ref, vp_ref = refs[:2]
        refs = refs[2:]
    lat_ref, latt_ref, upq_ref = refs[:3]
    refs = refs[3:]
    if chained:
        up_in = refs[2]
        refs = refs[3:]
    out_ref, bq_ref, upt_ref, dv_ref = refs[:4]
    refs = refs[4:]
    if far:
        dvp_ref = refs[0]
        refs = refs[1:]
    q_scr, dq_scr = refs

    tokens = qf_ref.shape[0]
    root = 1.0 / math.sqrt(WIDTH)
    base2 = root * math.log2(math.e)
    lat = lat_ref[:, :RANK]
    q_scr[...] = (qf_ref[...].astype(F32) + adapter_scale * dot(lat, upq_ref[...])).astype(BF16)
    if far:
        keys = jnp.concatenate([kp_ref[...], k_ref[...]], axis=0)
        values = jnp.concatenate([vp_ref[...], v_ref[...]], axis=0)
    else:
        keys = k_ref[...]
        values = v_ref[...]
    row = lax.broadcasted_iota(jnp.int32, (STACK * tokens, tokens), 0) % tokens
    col = lax.broadcasted_iota(jnp.int32, (STACK * tokens, tokens), 1)
    seen = col <= row
    dvt = None
    for block in range(PER_KEY // STACK):
        slices = [slice((block * STACK + n) * WIDTH, (block * STACK + n + 1) * WIDTH) for n in range(STACK)]
        q = jnp.concatenate([q_scr[:, cols] for cols in slices], axis=0)
        do = jnp.concatenate([do_ref[:, cols] for cols in slices], axis=0)
        score = dot_nt(q, keys)
        own = jnp.where(seen, score[:, -tokens:], masked_score)
        if far:
            score = jnp.concatenate([score[:, :tokens], own], axis=1)
        else:
            score = own
        top = jnp.max(score, axis=1, keepdims=True)
        expo = jnp.exp2((score - top) * base2)
        prob = expo * (1.0 / jnp.sum(expo, axis=1, keepdims=True))
        prob_b = prob.astype(BF16)
        if far:
            attended = dot(prob_b, values)
            dprob = dot_nt(do, values)
        else:
            dprob = dot_nt(do, values)
            attended = dot(prob_b, values)
        delta = jnp.sum(do.astype(F32) * attended, axis=1, keepdims=True)
        dscore = (prob * (dprob - delta)).astype(BF16)
        dq_rows = (dot(dscore, keys) * root).astype(BF16)
        for n, cols in enumerate(slices):
            rows = slice(n * tokens, (n + 1) * tokens)
            out_ref[:, cols] = attended[rows].astype(BF16)
            dq_scr[:, cols] = dq_rows[rows]
        term = lax.dot_general(do, prob_b, (((0,), (0,)), ((), ())), preferred_element_type=F32)
        dvt = term if dvt is None else dvt + term
    dv = dvt.T
    dv_ref[...] = dv[-tokens:]
    if far:
        dvp_ref[...] = dv[:tokens].astype(dvp_ref.dtype)
    dq = dq_scr[...]
    bq_ref[...] = dot(latt_ref[:RANK, :], dq)
    up = dot_nt(upq_ref[...], dq)
    step = pl.program_id(0)

    @pl.when(step == 0)
    def _():
        upt_ref[...] = up + up_in[...] if chained else up

    @pl.when(step > 0)
    def _():
        upt_ref[...] += up


def attend(first, groups, query_frozen, dout, keys, values, prev, lat, latt, up_q, chain):
    tokens = query_frozen.shape[0]
    far = prev is not None
    chained = chain is not None
    wide = PER_KEY * WIDTH
    at_group = lambda i, s: (0, s[0] + i)
    at_step = lambda i, s: (0, i)
    whole = lambda i, s: (0, 0)
    args = [query_frozen, dout, keys, values]
    specs = [
        pl.BlockSpec((tokens, wide), at_group),
        pl.BlockSpec((tokens, wide), at_group),
        pl.BlockSpec((tokens, WIDTH), at_group),
        pl.BlockSpec((tokens, WIDTH), at_group),
    ]
    if far:
        args += list(prev)
        specs += [pl.BlockSpec((tokens, WIDTH), at_group), pl.BlockSpec((tokens, WIDTH), at_step)]
    args += [lat, latt, up_q]
    specs += [
        pl.BlockSpec((tokens, 2 * RANK), whole),
        pl.BlockSpec((2 * RANK, tokens), whole),
        pl.BlockSpec((RANK, wide), at_group),
    ]
    aliases = {}
    if chained:
        aliases = {1 + len(args): 0, 2 + len(args): 1}
        args += list(chain)
        specs += [pl.BlockSpec(memory_space=pl.ANY)] * 2 + [pl.BlockSpec((RANK, tokens), whole)]
    out_specs = [
        pl.BlockSpec((tokens, wide), at_group),
        pl.BlockSpec((RANK, wide), at_group),
        pl.BlockSpec((RANK, tokens), whole),
        pl.BlockSpec((tokens, WIDTH), at_step),
    ]
    out_shape = [
        jax.ShapeDtypeStruct(query_frozen.shape, BF16),
        jax.ShapeDtypeStruct(up_q.shape, F32),
        jax.ShapeDtypeStruct((RANK, tokens), F32),
        jax.ShapeDtypeStruct((tokens, groups * WIDTH), F32),
    ]
    if far:
        out_specs.append(pl.BlockSpec((tokens, WIDTH), at_step))
        out_shape.append(jax.ShapeDtypeStruct((tokens, groups * WIDTH), BF16))
    span = tokens * (2 if far else 1)
    return pl.pallas_call(
        functools.partial(attend_kernel, far, chained),
        grid_spec=pltpu.PrefetchScalarGridSpec(
            num_scalar_prefetch=1,
            grid=(groups,),
            in_specs=specs,
            out_specs=out_specs,
            scratch_shapes=[pltpu.VMEM((tokens, wide), BF16), pltpu.VMEM((tokens, wide), BF16)],
        ),
        out_shape=out_shape,
        input_output_aliases=aliases,
        compiler_params=pltpu.CompilerParams(vmem_limit_bytes=VMEM_LIMIT),
        cost_estimate=pl.CostEstimate(
            flops=groups * 10 * tokens * span * wide,
            bytes_accessed=groups * 6 * tokens * wide,
            transcendentals=groups * PER_KEY * tokens * span,
        ),
        name="attend_far" if far else "attend_near",
    )(first, *args)


def outer_kernel(fresh, half_ref, *refs):
    refs = list(refs)
    x_ref, bq_ref, latt_ref, dv_ref = refs[:4]
    refs = refs[4:]
    if fresh:
        upt_ref, near_ref, back_ref, upv_far, upv_near, out_ref, both_ref, near_out, bv_scr = refs
    else:
        both_ref, out_ref, bv_scr = refs
    step = pl.program_id(0)

    @pl.when(step == 0)
    def _():
        dvb = dv_ref[...].astype(BF16)
        bv_scr[...] = dot(latt_ref[RANK:, :], dvb)
        if fresh:
            near = (near_ref[...] + back_ref[...].astype(F32)).astype(BF16)
            near_out[...] = near
            upv = dot_nt(upv_far[...], dvb) + dot_nt(upv_near[...], near)
            both_ref[...] = jnp.concatenate([upt_ref[...], upv], axis=0).astype(BF16)

    part = dot(both_ref[...], x_ref[...])
    for chunk in range(out_ref.shape[0]):
        for lane in range(2):
            cols = slice((2 * chunk + lane) * WIDTH, (2 * chunk + lane + 1) * WIDTH)
            rows = slice(lane * RANK, (lane + 1) * RANK)
            out_ref[chunk, rows, :] = part[:RANK, cols].astype(out_ref.dtype)
            rows = slice((2 + lane) * RANK, (3 + lane) * RANK)
            out_ref[chunk, rows, :] = part[RANK:, cols].astype(out_ref.dtype)
        cols = slice(chunk * WIDTH, (chunk + 1) * WIDTH)
        out_ref[chunk, 4 * RANK : 5 * RANK, :] = bq_ref[:, cols].astype(out_ref.dtype)
        out_ref[chunk, 5 * RANK :, :] = jnp.zeros((RANK, WIDTH), out_ref.dtype)

    @pl.when(step == 0)
    def _():
        for chunk in range(2):
            cols = slice(chunk * WIDTH, (chunk + 1) * WIDTH)
            out_ref[chunk, 5 * RANK :, :] = bv_scr[:, cols].astype(out_ref.dtype)


def outer(half, x, bq, latt, dv, dtype, fresh=None, both=None, steps=4):
    tokens, model = x.shape
    per_step = CHUNKS // 2 // steps
    along = lambda i, s: (0, s[0] * steps + i)
    whole = lambda i, s: (0, 0)
    cols = dv.shape[1]
    args = [x, bq, latt, dv]
    specs = [
        pl.BlockSpec((tokens, per_step * 2 * WIDTH), along),
        pl.BlockSpec((RANK, per_step * WIDTH), along),
        pl.BlockSpec((2 * RANK, tokens), whole),
        pl.BlockSpec((tokens, cols), whole),
    ]
    out_specs = [pl.BlockSpec((per_step, CHUNK_ROWS, WIDTH), lambda i, s: (i, 0, 0))]
    out_shape = [jax.ShapeDtypeStruct((CHUNKS // 2, CHUNK_ROWS, WIDTH), dtype)]
    if fresh is not None:
        upt, near, back, up_v = fresh
        args += [upt, near, back, up_v, up_v]
        specs += [
            pl.BlockSpec((RANK, tokens), whole),
            pl.BlockSpec((tokens, cols), whole),
            pl.BlockSpec((tokens, cols), whole),
            pl.BlockSpec((RANK, cols), lambda i, s: (0, s[0])),
            pl.BlockSpec((RANK, cols), lambda i, s: (0, 1 - s[0])),
        ]
        out_specs += [pl.BlockSpec((2 * RANK, tokens), whole), pl.BlockSpec((tokens, cols), whole)]
        out_shape += [
            jax.ShapeDtypeStruct((2 * RANK, tokens), BF16),
            jax.ShapeDtypeStruct((tokens, cols), BF16),
        ]
    else:
        args.append(both)
        specs.append(pl.BlockSpec((2 * RANK, tokens), whole))
    return pl.pallas_call(
        functools.partial(outer_kernel, fresh is not None),
        grid_spec=pltpu.PrefetchScalarGridSpec(
            num_scalar_prefetch=1,
            grid=(steps,),
            in_specs=specs,
            out_specs=out_specs,
            scratch_shapes=[pltpu.VMEM((RANK, cols), F32)],
        ),
        out_shape=out_shape,
        compiler_params=pltpu.CompilerParams(vmem_limit_bytes=VMEM_LIMIT),
        cost_estimate=pl.CostEstimate(
            flops=2 * tokens * model * RANK, bytes_accessed=tokens * model, transcendentals=0
        ),
        name="outer_first" if fresh is not None else "outer_second",
    )(half, *args)


def unpack_kernel(scale, half_ref, ref, *refs):
    aq_ref, av_ref, bq_ref, bv_ref = refs[-4:]
    for chunk in range(CHUNKS // 2):
        for lane in range(2):
            cols = slice((2 * chunk + lane) * WIDTH, (2 * chunk + lane + 1) * WIDTH)
            rows = slice(lane * RANK, (lane + 1) * RANK)
            aq_ref[:, cols] = ref[chunk, rows, :].astype(F32) * scale
            rows = slice((2 + lane) * RANK, (3 + lane) * RANK)
            av_ref[:, cols] = ref[chunk, rows, :].astype(F32) * scale
        cols = slice(chunk * WIDTH, (chunk + 1) * WIDTH)
        bq_ref[:, cols] = ref[chunk, 4 * RANK : 5 * RANK, :].astype(F32) * scale
        if chunk < 2:
            bv_ref[:, cols] = ref[chunk, 5 * RANK :, :].astype(F32) * scale


def unpacked(half, chunks, scale, shapes, filled=()):
    at_half = lambda i, s: (0, s[0])
    return pl.pallas_call(
        functools.partial(unpack_kernel, scale),
        grid_spec=pltpu.PrefetchScalarGridSpec(
            num_scalar_prefetch=1,
            grid=(1,),
            in_specs=[pl.BlockSpec(chunks.shape, lambda i, s: (0, 0, 0))]
            + [pl.BlockSpec(memory_space=pl.ANY)] * len(filled),
            out_specs=[pl.BlockSpec((rows, cols // 2), at_half) for rows, cols in shapes],
        ),
        out_shape=[jax.ShapeDtypeStruct(shape, F32) for shape in shapes],
        input_output_aliases={2 + n: n for n in range(len(filled))},
        compiler_params=pltpu.CompilerParams(vmem_limit_bytes=VMEM_LIMIT),
        cost_estimate=pl.CostEstimate(flops=0, bytes_accessed=1024 * 1024, transcendentals=0),
        name="unpack_other" if filled else "unpack_own",
    )(half, chunks, *filled)


def summed(given, kept):
    halves = kept + swapped(given, CORE_BIT).astype(F32)
    piece = sum_over_first(exchanged(halves.astype(BF16), PLANE_BITS))
    for bits in DEPTH_STEPS:
        mine = piece.astype(BF16)
        piece = mine.astype(F32) + swapped(mine, bits).astype(F32)
    return spread(piece.astype(BF16), PLANE_BITS)


def on_device(
    normed,
    query_frozen,
    key_projected,
    value_frozen,
    query_down_weight,
    query_up_weight,
    value_down_weight,
    value_up_weight,
    output_cotangent,
):
    x, qf, keys, vf, dout = [
        a[0] for a in (normed, query_frozen, key_projected, value_frozen, output_cotangent)
    ]
    tokens = x.shape[0]
    parity = lax.axis_index("seq") % 2
    place = parity.reshape(1).astype(jnp.int32)
    away = 1 - place
    pair = KEY_VALUE_HEADS // 2
    prev_keys = shifted(keys, "seq", 1)
    lat, latt, values, sent = latents(
        place, x, query_down_weight.T, value_down_weight.T, vf, value_up_weight
    )
    prev = (prev_keys, shifted(sent, "seq", 1))
    out, bq, upt, dv_near = attend(
        pair * place, pair, qf, dout, keys, values, None, lat, latt, query_up_weight, None
    )
    out, bq, upt, dv_far, dv_back = attend(
        pair * away, pair, qf, dout, keys, values, prev, lat, latt, query_up_weight, (out, bq, upt)
    )
    back = shifted(dv_back, "seq", -1)
    given, both, near = outer(
        away, x, bq, latt, dv_far, BF16, fresh=(upt, dv_near, back, value_up_weight)
    )
    (kept,) = outer(place, x, bq, latt, near, F32, both=both)
    own_half = summed(given, kept)
    other_half = swapped(own_half, CORE_BIT)
    scale_factor = adapter_scale / math.sqrt(tokens * lax.axis_size("seq") * lax.axis_size("dp"))
    model = x.shape[1]
    shapes = [(RANK, model), (RANK, model), (RANK, qf.shape[1]), (RANK, vf.shape[1])]
    first_half = unpacked(place, own_half, scale_factor, shapes)
    aq, av, bq_sum, bv_sum = unpacked(away, other_half, scale_factor, shapes, first_half)
    return (out[None], aq.T, bq_sum, av.T, bv_sum)


def solution(mesh):
    in_specs = (
        P("dp", "seq", None),
        P("dp", "seq", None),
        P("dp", "seq", None),
        P("dp", "seq", None),
        P(),
        P(),
        P(),
        P(),
        P("dp", "seq", None),
    )
    out_specs = (P("dp", "seq", None), P(), P(), P(), P())
    return jax.shard_map(
        on_device, mesh=mesh, in_specs=in_specs, out_specs=out_specs, check_vma=False
    )
```

```python
import functools
import math

import jax
import jax.numpy as jnp
from jax import lax
from jax.experimental import pallas as pl
from jax.experimental.pallas import tpu as pltpu
from jax.sharding import PartitionSpec as P

QUERY_HEADS = 32
KEY_VALUE_HEADS = 4
PER_KEY = 8
WIDTH = 128
RANK = 16
adapter_scale = 2.0
masked_score = -1e30
AXES = ("seq", "dp")
CORE_BIT = 16
PLANE_BITS = (128, 8, 32, 64)
DEPTH_STEPS = (1, 2, 6)
CHUNKS = 32
CHUNK_ROWS = 96
NT = (((1,), (1,)), ((), ()))
F32 = jnp.float32
BF16 = jnp.bfloat16
STACK = 4
VMEM_LIMIT = 48 * 1024 * 1024


def groups_of(bits, count):
    groups = []
    for base in range(count):
        if any(base & bit for bit in bits):
            continue
        members = []
        for code in range(1 << len(bits)):
            members.append(base + sum(bit for n, bit in enumerate(bits) if code >> n & 1))
        groups.append(members)
    return groups


def exchanged(value, bits):
    groups = groups_of(bits, lax.axis_size(AXES))
    return lax.all_to_all(value, AXES, 0, 0, axis_index_groups=groups)


def sum_over_first(value):
    return jnp.sum(value.astype(jnp.float32), axis=0)


def spread(value, bits):
    copies = jnp.broadcast_to(value[None], (1 << len(bits),) + value.shape)
    return exchanged(copies, bits)


def swapped(value, bit):
    count = lax.axis_size(AXES)
    return lax.ppermute(value, AXES, [(i, i ^ bit) for i in range(count)])


def shifted(value, axis, by):
    devices = lax.axis_size(axis)
    return lax.ppermute(value, axis, [(i, (i + by) % devices) for i in range(devices)])


def dot_nt(a, b):
    return lax.dot_general(a, b, NT, preferred_element_type=F32)


def dot(a, b):
    return jnp.dot(a, b, preferred_element_type=F32)


def in_hbm(value):
    return pltpu.with_memory_space_constraint(value, pltpu.HBM)


def latent_kernel(steps, place_ref, x_hbm, dq_hbm, dv_hbm, vf_hbm, upv_hbm, lat_ref, latt_ref, value_ref, send_ref, x_buf, down, vf_buf, up_buf, sems):
    tokens, model = x_buf.shape
    block = model // steps
    first = [
        pltpu.make_async_copy(dq_hbm, down.at[pl.ds(0, RANK)], sems.at[steps]),
        pltpu.make_async_copy(dv_hbm, down.at[pl.ds(RANK, RANK)], sems.at[steps + 1]),
    ]
    last = [
        pltpu.make_async_copy(vf_hbm, vf_buf, sems.at[steps + 2]),
        pltpu.make_async_copy(upv_hbm, up_buf, sems.at[steps + 3]),
    ]
    pieces = []
    for step in range(steps):
        cols = pl.ds(step * block, block)
        pieces.append(pltpu.make_async_copy(x_hbm.at[:, cols], x_buf.at[:, cols], sems.at[step]))
    for copy in first + pieces + last:
        copy.start()
    for copy in first:
        copy.wait()
    whole = None
    for step in range(steps):
        pieces[step].wait()
        cols = slice(step * block, (step + 1) * block)
        part = dot_nt(x_buf[:, cols], down[:, cols])
        whole = part if whole is None else whole + part
    for copy in last:
        copy.wait()
    lat = whole.astype(BF16)
    lat_ref[...] = lat
    latt_ref[...] = whole.T.astype(BF16)
    up = dot(lat[:, RANK:], up_buf[...])
    value_ref[...] = (vf_buf[...].astype(F32) + adapter_scale * up).astype(BF16)
    half = value_ref.shape[1] // 2
    send_ref[...] = value_ref[:, pl.ds(pl.multiple_of(place_ref[0] * half, half), half)]


def latents(place, x, down_q, down_v, value_frozen, up_v, steps=8):
    tokens, model = x.shape
    cols = value_frozen.shape[1]
    whole = lambda i, s: (0, 0)
    return pl.pallas_call(
        functools.partial(latent_kernel, steps),
        grid_spec=pltpu.PrefetchScalarGridSpec(
            num_scalar_prefetch=1,
            grid=(1,),
            in_specs=[pl.BlockSpec(memory_space=pl.ANY)] * 5,
            out_specs=[
                pl.BlockSpec((tokens, 2 * RANK), whole),
                pl.BlockSpec((2 * RANK, tokens), whole),
                pl.BlockSpec((tokens, cols), whole),
                pl.BlockSpec((tokens, cols // 2), whole),
            ],
            scratch_shapes=[
                pltpu.VMEM((tokens, model), BF16),
                pltpu.VMEM((2 * RANK, model), BF16),
                pltpu.VMEM((tokens, cols), BF16),
                pltpu.VMEM((RANK, cols), BF16),
                pltpu.SemaphoreType.DMA((steps + 4,)),
            ],
        ),
        out_shape=[
            jax.ShapeDtypeStruct((tokens, 2 * RANK), BF16),
            jax.ShapeDtypeStruct((2 * RANK, tokens), BF16),
            jax.ShapeDtypeStruct((tokens, cols), BF16),
            jax.ShapeDtypeStruct((tokens, cols // 2), BF16),
        ],
        compiler_params=pltpu.CompilerParams(vmem_limit_bytes=48 * 1024 * 1024),
        cost_estimate=pl.CostEstimate(
            flops=2 * tokens * model * 2 * RANK, bytes_accessed=2 * tokens * model, transcendentals=0
        ),
        name="latents",
    )(place, *[in_hbm(a) for a in (x, down_q, down_v, value_frozen, up_v)])


def attend_kernel(far, chained, first_ref, *refs):
    refs = list(refs)
    qf_ref, do_ref, k_ref, v_ref = refs[:4]
    refs = refs[4:]
    if far:
        kp_ref, vp_ref = refs[:2]
        refs = refs[2:]
    lat_ref, latt_ref, upq_ref = refs[:3]
    refs = refs[3:]
    if chained:
        up_in = refs[2]
        refs = refs[3:]
    out_ref, bq_ref, upt_ref, dv_ref = refs[:4]
    refs = refs[4:]
    if far:
        dvp_ref = refs[0]
        refs = refs[1:]
    q_scr, dq_scr = refs

    tokens = qf_ref.shape[0]
    root = 1.0 / math.sqrt(WIDTH)
    base2 = root * math.log2(math.e)
    lat = lat_ref[:, :RANK]
    q_scr[...] = (qf_ref[...].astype(F32) + adapter_scale * dot(lat, upq_ref[...])).astype(BF16)
    if far:
        keys = jnp.concatenate([kp_ref[...], k_ref[...]], axis=0)
        values = jnp.concatenate([vp_ref[...], v_ref[...]], axis=0)
    else:
        keys = k_ref[...]
        values = v_ref[...]
    row = lax.broadcasted_iota(jnp.int32, (STACK * tokens, tokens), 0) % tokens
    col = lax.broadcasted_iota(jnp.int32, (STACK * tokens, tokens), 1)
    seen = col <= row
    dvt = None
    for block in range(PER_KEY // STACK):
        slices = [slice((block * STACK + n) * WIDTH, (block * STACK + n + 1) * WIDTH) for n in range(STACK)]
        q = jnp.concatenate([q_scr[:, cols] for cols in slices], axis=0)
        do = jnp.concatenate([do_ref[:, cols] for cols in slices], axis=0)
        score = dot_nt(q, keys)
        own = jnp.where(seen, score[:, -tokens:], masked_score)
        if far:
            score = jnp.concatenate([score[:, :tokens], own], axis=1)
        else:
            score = own
        top = jnp.max(score, axis=1, keepdims=True)
        expo = jnp.exp2((score - top) * base2)
        prob = expo * (1.0 / jnp.sum(expo, axis=1, keepdims=True))
        prob_b = prob.astype(BF16)
        if far:
            attended = dot(prob_b, values)
            dprob = dot_nt(do, values)
        else:
            dprob = dot_nt(do, values)
            attended = dot(prob_b, values)
        delta = jnp.sum(do.astype(F32) * attended, axis=1, keepdims=True)
        dscore = (prob * (dprob - delta)).astype(BF16)
        dq_rows = (dot(dscore, keys) * root).astype(BF16)
        for n, cols in enumerate(slices):
            rows = slice(n * tokens, (n + 1) * tokens)
            out_ref[:, cols] = attended[rows].astype(BF16)
            dq_scr[:, cols] = dq_rows[rows]
        term = lax.dot_general(do, prob_b, (((0,), (0,)), ((), ())), preferred_element_type=F32)
        dvt = term if dvt is None else dvt + term
    dv = dvt.T
    dv_ref[...] = dv[-tokens:]
    if far:
        dvp_ref[...] = dv[:tokens].astype(dvp_ref.dtype)
    dq = dq_scr[...]
    bq_ref[...] = dot(latt_ref[:RANK, :], dq)
    up = dot_nt(upq_ref[...], dq)
    step = pl.program_id(0)

    @pl.when(step == 0)
    def _():
        upt_ref[...] = up + up_in[...] if chained else up

    @pl.when(step > 0)
    def _():
        upt_ref[...] += up


def attend(first, groups, query_frozen, dout, keys, values, prev, lat, latt, up_q, chain):
    tokens = query_frozen.shape[0]
    far = prev is not None
    chained = chain is not None
    wide = PER_KEY * WIDTH
    at_group = lambda i, s: (0, s[0] + i)
    at_step = lambda i, s: (0, i)
    whole = lambda i, s: (0, 0)
    args = [query_frozen, dout, keys, values]
    specs = [
        pl.BlockSpec((tokens, wide), at_group),
        pl.BlockSpec((tokens, wide), at_group),
        pl.BlockSpec((tokens, WIDTH), at_group),
        pl.BlockSpec((tokens, WIDTH), at_group),
    ]
    if far:
        args += list(prev)
        specs += [pl.BlockSpec((tokens, WIDTH), at_group), pl.BlockSpec((tokens, WIDTH), at_step)]
    args += [lat, latt, up_q]
    specs += [
        pl.BlockSpec((tokens, 2 * RANK), whole),
        pl.BlockSpec((2 * RANK, tokens), whole),
        pl.BlockSpec((RANK, wide), at_group),
    ]
    aliases = {}
    if chained:
        aliases = {1 + len(args): 0, 2 + len(args): 1}
        args += list(chain)
        specs += [pl.BlockSpec(memory_space=pl.ANY)] * 2 + [pl.BlockSpec((RANK, tokens), whole)]
    out_specs = [
        pl.BlockSpec((tokens, wide), at_group),
        pl.BlockSpec((RANK, wide), at_group),
        pl.BlockSpec((RANK, tokens), whole),
        pl.BlockSpec((tokens, WIDTH), at_step),
    ]
    out_shape = [
        jax.ShapeDtypeStruct(query_frozen.shape, BF16),
        jax.ShapeDtypeStruct(up_q.shape, F32),
        jax.ShapeDtypeStruct((RANK, tokens), F32),
        jax.ShapeDtypeStruct((tokens, groups * WIDTH), F32),
    ]
    if far:
        out_specs.append(pl.BlockSpec((tokens, WIDTH), at_step))
        out_shape.append(jax.ShapeDtypeStruct((tokens, groups * WIDTH), BF16))
    span = tokens * (2 if far else 1)
    return pl.pallas_call(
        functools.partial(attend_kernel, far, chained),
        grid_spec=pltpu.PrefetchScalarGridSpec(
            num_scalar_prefetch=1,
            grid=(groups,),
            in_specs=specs,
            out_specs=out_specs,
            scratch_shapes=[pltpu.VMEM((tokens, wide), BF16), pltpu.VMEM((tokens, wide), BF16)],
        ),
        out_shape=out_shape,
        input_output_aliases=aliases,
        compiler_params=pltpu.CompilerParams(vmem_limit_bytes=VMEM_LIMIT),
        cost_estimate=pl.CostEstimate(
            flops=groups * 10 * tokens * span * wide,
            bytes_accessed=groups * 6 * tokens * wide,
            transcendentals=groups * PER_KEY * tokens * span,
        ),
        name="attend_far" if far else "attend_near",
    )(first, *args)


def outer_kernel(fresh, half_ref, *refs):
    refs = list(refs)
    x_ref, bq_ref, latt_ref, dv_ref = refs[:4]
    refs = refs[4:]
    if fresh:
        upt_ref, near_ref, back_ref, upv_far, upv_near, out_ref, both_ref, near_out, bv_scr = refs
    else:
        both_ref, out_ref, bv_scr = refs
    step = pl.program_id(0)

    @pl.when(step == 0)
    def _():
        dvb = dv_ref[...].astype(BF16)
        bv_scr[...] = dot(latt_ref[RANK:, :], dvb)
        if fresh:
            near = (near_ref[...] + back_ref[...].astype(F32)).astype(BF16)
            near_out[...] = near
            upv = dot_nt(upv_far[...], dvb) + dot_nt(upv_near[...], near)
            both_ref[...] = jnp.concatenate([upt_ref[...], upv], axis=0).astype(BF16)

    part = dot(both_ref[...], x_ref[...])
    for chunk in range(out_ref.shape[0]):
        for lane in range(2):
            cols = slice((2 * chunk + lane) * WIDTH, (2 * chunk + lane + 1) * WIDTH)
            rows = slice(lane * RANK, (lane + 1) * RANK)
            out_ref[chunk, rows, :] = part[:RANK, cols].astype(out_ref.dtype)
            rows = slice((2 + lane) * RANK, (3 + lane) * RANK)
            out_ref[chunk, rows, :] = part[RANK:, cols].astype(out_ref.dtype)
        cols = slice(chunk * WIDTH, (chunk + 1) * WIDTH)
        out_ref[chunk, 4 * RANK : 5 * RANK, :] = bq_ref[:, cols].astype(out_ref.dtype)
        out_ref[chunk, 5 * RANK :, :] = jnp.zeros((RANK, WIDTH), out_ref.dtype)

    @pl.when(step == 0)
    def _():
        for chunk in range(2):
            cols = slice(chunk * WIDTH, (chunk + 1) * WIDTH)
            out_ref[chunk, 5 * RANK :, :] = bv_scr[:, cols].astype(out_ref.dtype)


def outer(half, x, bq, latt, dv, dtype, fresh=None, both=None, steps=4):
    tokens, model = x.shape
    per_step = CHUNKS // 2 // steps
    along = lambda i, s: (0, s[0] * steps + i)
    whole = lambda i, s: (0, 0)
    cols = dv.shape[1]
    args = [x, bq, latt, dv]
    specs = [
        pl.BlockSpec((tokens, per_step * 2 * WIDTH), along),
        pl.BlockSpec((RANK, per_step * WIDTH), along),
        pl.BlockSpec((2 * RANK, tokens), whole),
        pl.BlockSpec((tokens, cols), whole),
    ]
    out_specs = [pl.BlockSpec((per_step, CHUNK_ROWS, WIDTH), lambda i, s: (i, 0, 0))]
    out_shape = [jax.ShapeDtypeStruct((CHUNKS // 2, CHUNK_ROWS, WIDTH), dtype)]
    if fresh is not None:
        upt, near, back, up_v = fresh
        args += [upt, near, back, up_v, up_v]
        specs += [
            pl.BlockSpec((RANK, tokens), whole),
            pl.BlockSpec((tokens, cols), whole),
            pl.BlockSpec((tokens, cols), whole),
            pl.BlockSpec((RANK, cols), lambda i, s: (0, s[0])),
            pl.BlockSpec((RANK, cols), lambda i, s: (0, 1 - s[0])),
        ]
        out_specs += [pl.BlockSpec((2 * RANK, tokens), whole), pl.BlockSpec((tokens, cols), whole)]
        out_shape += [
            jax.ShapeDtypeStruct((2 * RANK, tokens), BF16),
            jax.ShapeDtypeStruct((tokens, cols), BF16),
        ]
    else:
        args.append(both)
        specs.append(pl.BlockSpec((2 * RANK, tokens), whole))
    return pl.pallas_call(
        functools.partial(outer_kernel, fresh is not None),
        grid_spec=pltpu.PrefetchScalarGridSpec(
            num_scalar_prefetch=1,
            grid=(steps,),
            in_specs=specs,
            out_specs=out_specs,
            scratch_shapes=[pltpu.VMEM((RANK, cols), F32)],
        ),
        out_shape=out_shape,
        compiler_params=pltpu.CompilerParams(vmem_limit_bytes=VMEM_LIMIT),
        cost_estimate=pl.CostEstimate(
            flops=2 * tokens * model * RANK, bytes_accessed=tokens * model, transcendentals=0
        ),
        name="outer_first" if fresh is not None else "outer_second",
    )(half, *args)


def unpack_kernel(scale, half_ref, ref, *refs):
    aq_ref, av_ref, bq_ref, bv_ref = refs[-4:]
    for chunk in range(CHUNKS // 2):
        for lane in range(2):
            cols = slice((2 * chunk + lane) * WIDTH, (2 * chunk + lane + 1) * WIDTH)
            rows = slice(lane * RANK, (lane + 1) * RANK)
            aq_ref[:, cols] = ref[chunk, rows, :].astype(F32) * scale
            rows = slice((2 + lane) * RANK, (3 + lane) * RANK)
            av_ref[:, cols] = ref[chunk, rows, :].astype(F32) * scale
        cols = slice(chunk * WIDTH, (chunk + 1) * WIDTH)
        bq_ref[:, cols] = ref[chunk, 4 * RANK : 5 * RANK, :].astype(F32) * scale
        if chunk < 2:
            bv_ref[:, cols] = ref[chunk, 5 * RANK :, :].astype(F32) * scale


def unpacked(half, chunks, scale, shapes, filled=()):
    at_half = lambda i, s: (0, s[0])
    return pl.pallas_call(
        functools.partial(unpack_kernel, scale),
        grid_spec=pltpu.PrefetchScalarGridSpec(
            num_scalar_prefetch=1,
            grid=(1,),
            in_specs=[pl.BlockSpec(chunks.shape, lambda i, s: (0, 0, 0))]
            + [pl.BlockSpec(memory_space=pl.ANY)] * len(filled),
            out_specs=[pl.BlockSpec((rows, cols // 2), at_half) for rows, cols in shapes],
        ),
        out_shape=[jax.ShapeDtypeStruct(shape, F32) for shape in shapes],
        input_output_aliases={2 + n: n for n in range(len(filled))},
        compiler_params=pltpu.CompilerParams(vmem_limit_bytes=VMEM_LIMIT),
        cost_estimate=pl.CostEstimate(flops=0, bytes_accessed=1024 * 1024, transcendentals=0),
        name="unpack_other" if filled else "unpack_own",
    )(half, chunks, *filled)


def summed(given, kept):
    halves = kept + swapped(given, CORE_BIT).astype(F32)
    piece = sum_over_first(exchanged(halves.astype(BF16), PLANE_BITS))
    for bits in DEPTH_STEPS:
        mine = piece.astype(BF16)
        piece = mine.astype(F32) + swapped(mine, bits).astype(F32)
    return spread(piece.astype(BF16), PLANE_BITS)


def on_device(
    normed,
    query_frozen,
    key_projected,
    value_frozen,
    query_down_weight,
    query_up_weight,
    value_down_weight,
    value_up_weight,
    output_cotangent,
):
    x, qf, keys, vf, dout = [
        a[0] for a in (normed, query_frozen, key_projected, value_frozen, output_cotangent)
    ]
    tokens = x.shape[0]
    parity = lax.axis_index("seq") % 2
    place = parity.reshape(1).astype(jnp.int32)
    away = 1 - place
    pair = KEY_VALUE_HEADS // 2
    prev_keys = shifted(keys, "seq", 1)
    lat, latt, values, sent = latents(
        place, x, query_down_weight.T, value_down_weight.T, vf, value_up_weight
    )
    prev = (prev_keys, shifted(sent, "seq", 1))
    out, bq, upt, dv_near = attend(
        pair * place, pair, qf, dout, keys, values, None, lat, latt, query_up_weight, None
    )
    out, bq, upt, dv_far, dv_back = attend(
        pair * away, pair, qf, dout, keys, values, prev, lat, latt, query_up_weight, (out, bq, upt)
    )
    back = shifted(dv_back, "seq", -1)
    given, both, near = outer(
        away, x, bq, latt, dv_far, BF16, fresh=(upt, dv_near, back, value_up_weight)
    )
    (kept,) = outer(place, x, bq, latt, near, F32, both=both)
    own_half = summed(given, kept)
    other_half = swapped(own_half, CORE_BIT)
    scale_factor = adapter_scale / math.sqrt(tokens * lax.axis_size("seq") * lax.axis_size("dp"))
    model = x.shape[1]
    shapes = [(RANK, model), (RANK, model), (RANK, qf.shape[1]), (RANK, vf.shape[1])]
    first_half = unpacked(place, own_half, scale_factor, shapes)
    aq, av, bq_sum, bv_sum = unpacked(away, other_half, scale_factor, shapes, first_half)
    return (out[None], aq.T, bq_sum, av.T, bv_sum)


def solution(mesh):
    in_specs = (
        P("dp", "seq", None),
        P("dp", "seq", None),
        P("dp", "seq", None),
        P("dp", "seq", None),
        P(),
        P(),
        P(),
        P(),
        P("dp", "seq", None),
    )
    out_specs = (P("dp", "seq", None), P(), P(), P(), P())
    return jax.shard_map(
        on_device, mesh=mesh, in_specs=in_specs, out_specs=out_specs, check_vma=False
    )
```
